32 devices in a mesh: parts: 2 (over y), seq: 4 (over z), chan: 4 (over x, core).
Axes of the slice: x: 2, y: 2, z: 4, core: 2. Of those that a mesh axis runs over, the one named last changes fastest.
Arguments:
- records: bfloat16 [8, 1536, 512], P('parts', 'seq', 'chan'), parts along dimension 0, may hold values from -6 to 6
- norm_gain: float32 [512], replicated, may hold values from 0.1 to 1.9
- in_projection: bfloat16 [512, 3, 512], P(None, None, 'chan'), may hold values from -0.25 to 0.25
- short_kernel: float32 [3, 3, 512], P(None, None, 'chan'), may hold values from -3.5 to 3.5
- long_filter: bfloat16 [16, 1536], P('chan', 'seq'), may hold values from -1.6 to 1.6
- skip_gain: float32 [512], P('chan'), may hold values from 0.5 to 1.5
- out_projection: bfloat16 [512, 512], P('chan'), may hold values from -0.25 to 0.25
Outputs:
- mixed: bfloat16 [8, 1536, 512], P('parts', 'seq', 'chan'), parts along dimension 0
The draws below stay inside these ranges and needn't reach their ends.
There are 2 independent parts, one for each index of `parts`. The reference program is written for one: setup_inputs(seed, part) draws one part's arguments, and reference() takes and returns one part's arrays. A program takes and returns all parts, laid end to end along the dimension named above; an argument that names none is the same for every part. Nothing has to cross between parts.
All inputs are finite; a program needn't handle non-finite values.
Results may differ from the reference program's by a relative error of at most 0.015.
Values may be sent and summed in bfloat16 or wider, within the bound.
No kernel may reach another device: no remote copies, remote signals or barrier semaphores. Data moves between devices by JAX's collectives and lax.ppermute only.
A program may use at most 128 MiB of HBM per device.

```python
import jax
import jax.numpy as jnp
from jax import lax

D = 512
FGROUP = 32
RECS = 4
FILTERS = 16
LENGTH = 1536


def draw_long_filter(key, part):
    first_key, second_key, level_key, sign_key = jax.random.split(jax.random.fold_in(key, 11), 4)
    picked = jax.random.uniform(first_key, (FILTERS, 1), dtype=jnp.float32)
    reach = jnp.exp(jnp.log(20.0) + picked * (jnp.log(4.0 * LENGTH) - jnp.log(20.0)))
    noise = jnp.clip(jax.random.normal(second_key, (FILTERS, LENGTH), dtype=jnp.float32), -5.0, 5.0)
    lags = jnp.arange(LENGTH, dtype=jnp.float32)[None, :]
    amplitude = 1.0 / jnp.sqrt(jnp.minimum(0.5 * reach + 1.0, LENGTH * 1.0))
    magnitude = jax.random.uniform(level_key, (FILTERS, 1), dtype=jnp.float32, minval=1.5, maxval=3.0)
    signs = jax.random.bernoulli(sign_key, 0.5, (FILTERS, 1)).astype(jnp.float32) * 2.0 - 1.0
    tail_part = magnitude * signs / LENGTH * jnp.exp(-lags / (3.0 * LENGTH))
    return (noise * jnp.exp(-lags / reach) * amplitude + tail_part).astype(jnp.bfloat16)


def draw_records(key, part):
    common_key, noise_key = jax.random.split(jax.random.fold_in(key, 23), 2)
    common = jax.random.normal(common_key, (RECS, 1, D), dtype=jnp.float32)
    noise = jnp.clip(jax.random.normal(noise_key, (RECS, LENGTH, D), dtype=jnp.float32), -5.0, 5.0)
    values = 0.8 * common + 0.8 * noise
    return jnp.clip(values, -6.0, 6.0).astype(jnp.bfloat16)


def levels(stream_key, shape, pieces, smallest, largest):
    def one(dim, shards_of):
        steps = jax.random.uniform(jax.random.fold_in(jax.random.fold_in(stream_key, 6), dim), (shards_of,), jnp.float32, smallest / len(pieces), largest / len(pieces))
        return jnp.repeat(jnp.exp(steps), shape[dim] // shards_of).reshape((-1,) + (1,) * (len(shape) - dim - 1))

    level = one(*pieces[0])
    for cut in pieces[1:]:
        level = level * one(*cut)
    return level


def bell_draw(stream_key, shape, width, most, cuts=(), kind=jnp.bfloat16):
    entries = jax.random.normal(stream_key, shape, jnp.float32) * width
    if len(cuts) > 0:
        entries = levels(stream_key, shape, cuts, -0.22, 0.18) * entries
    return jnp.clip(entries, min=-most, max=most).astype(kind)


def setup_inputs(seed: int = 0, part: int = 0) -> dict:
    key_list = jax.random.split(jax.random.key(seed), 8)
    part_keys = jax.random.split(jax.random.fold_in(key_list[7], part), 8)
    return {
        "records": draw_records(jax.random.fold_in(jax.random.fold_in(key_list[7], part), 71), part),
        "norm_gain": jnp.clip(1.0 + 0.18 * jax.random.normal(key_list[1], (D,), jnp.float32), 0.1, 1.9),
        "in_projection": bell_draw(key_list[2], (D, 3, D), D ** -0.5, 0.25, ((2, 4),)),
        "short_kernel": bell_draw(key_list[3], (3, 3, D), 3 ** -0.5, 3.5, ((2, 4),), jnp.float32),
        "long_filter": draw_long_filter(jax.random.fold_in(key_list[7], 71), part),
        "skip_gain": jnp.clip(0.5 + 1.0 * jax.random.uniform(key_list[5], (D,), jnp.float32) ** levels(key_list[5], (D,), ((0, 4),), -0.2, 0.2), 0.5, 1.5),
        "out_projection": bell_draw(key_list[6], (D, D), D ** -0.5, 0.25, ((0, 4),)),
    }


def reference(records, norm_gain, in_projection, short_kernel, long_filter, skip_gain, out_projection):
    widened = records.astype(jnp.float32)
    inv_rms = lax.rsqrt(lax.optimization_barrier(jnp.mean(widened * widened, axis=-1, keepdims=True)) + 1e-06)
    normed = (widened * inv_rms * norm_gain).astype(jnp.bfloat16)
    projected = jnp.einsum('rtd,dkc->rtkc', normed.astype(jnp.float32), in_projection.astype(jnp.float32)).astype(jnp.bfloat16)
    extended = jnp.pad(projected.astype(jnp.float32), ((0, 0), (2, 0), (0, 0), (0, 0)))
    streams = short_kernel[0] * extended[:, 2:] + short_kernel[1] * extended[:, 1:-1] + short_kernel[2] * extended[:, :-2]
    query_gate = streams[:, :, 0]
    gated_source = (streams[:, :, 1] * streams[:, :, 2]).astype(jnp.bfloat16)
    per_channel = jnp.repeat(long_filter.astype(jnp.float32), FGROUP, axis=0).T
    filter_spec = jnp.fft.rfft(per_channel, n=2 * LENGTH, axis=0)

    def convolve(signal):
        spectrum = jnp.fft.rfft(signal, n=2 * LENGTH, axis=0) * filter_spec
        return jnp.fft.irfft(spectrum, n=2 * LENGTH, axis=0)[:LENGTH]
    widened_source = gated_source.astype(jnp.float32)
    long_out = lax.map(convolve, widened_source) + skip_gain * widened_source
    gated = (query_gate * long_out).astype(jnp.bfloat16)
    mixed = jnp.einsum('rtc,cd->rtd', gated.astype(jnp.float32), out_projection.astype(jnp.float32))
    return mixed.astype(jnp.bfloat16)
```

```python
import jax
import jax.numpy as jnp
from jax import lax
from jax.experimental import pallas as pl
from jax.experimental.pallas import tpu as pltpu
from jax.sharding import PartitionSpec as P

LANES = 128
EXTRA = 32
BACK = 16
VMEM = pltpu.VMEM


def from_behind(block, axis, distance):
    devices = range(lax.axis_size(axis))
    route = [(i - distance, i) for i in devices if i - distance in devices]
    return lax.ppermute(block, axis, route)


def block_terms(taps_padded, offset, block_source, block_len):
    filter_count = taps_padded.shape[0]
    window = lax.dynamic_slice_in_dim(taps_padded, offset + 1, 2 * block_len - 1, 1)
    flipped = window[:, ::-1]
    padded = jnp.pad(flipped, ((0, 0), (0, 1)))
    tiled_taps = jnp.tile(padded, (1, block_len))
    toeplitz = tiled_taps[:, block_len - 1 : block_len - 1 + block_len * (2 * block_len - 1)]
    toeplitz = toeplitz.reshape(filter_count, block_len, 2 * block_len - 1)[:, :, :block_len]
    record_count = block_source.shape[0]
    grouped = block_source.reshape(record_count, block_len, filter_count, -1)
    return jnp.einsum("fab,rbfg->rafg", toeplitz, grouped, preferred_element_type=jnp.float32)


def ring_body(records, norm_gain, in_projection, short_kernel, long_filter, skip_gain, out_projection):
    gathered = lax.all_gather(records, "chan", axis=2, tiled=True)
    widened = gathered.astype(jnp.float32)
    inv_rms = lax.rsqrt(jnp.mean(widened * widened, axis=-1, keepdims=True) + 1e-06)
    normed = (widened * inv_rms * norm_gain).astype(jnp.bfloat16)
    projected = jnp.einsum(
        "rtd,dkc->rtkc", normed, in_projection, preferred_element_type=jnp.float32
    ).astype(jnp.bfloat16)
    rim_rows = from_behind(projected[:, -2:], "seq", 1)
    extended = jnp.concatenate([rim_rows, projected], axis=1).astype(jnp.float32)
    streams = (
        short_kernel[0] * extended[:, 2:]
        + short_kernel[1] * extended[:, 1:-1]
        + short_kernel[2] * extended[:, :-2]
    )
    query_gate = streams[:, :, 0]
    gated_source = (streams[:, :, 1] * streams[:, :, 2]).astype(jnp.bfloat16)
    record_count, block_len, channels = gated_source.shape
    all_taps = lax.all_gather(long_filter, "seq", axis=1, tiled=True)
    taps_padded = jnp.concatenate(
        [jnp.zeros((all_taps.shape[0], block_len), jnp.bfloat16), all_taps], axis=1
    )
    my_start = lax.axis_index("seq") * block_len
    cycle_stops = lax.axis_size("seq")
    long_sum = block_terms(taps_padded, 0, gated_source, block_len)

    def advance(stop_index, state):
        running_sum, visiting = state
        visiting = from_behind(visiting, "seq", 1)
        lag_start = stop_index * block_len
        running_sum = lax.cond(
            lag_start <= my_start,
            lambda running: running + block_terms(taps_padded, lag_start, visiting, block_len),
            lambda running: running,
            running_sum,
        )
        return (running_sum, visiting)

    long_sum, _ = lax.fori_loop(1, cycle_stops, advance, (long_sum, gated_source))
    long_out = long_sum.reshape(
        record_count, block_len, channels
    ) + skip_gain * gated_source.astype(jnp.float32)
    gated = (query_gate * long_out).astype(jnp.bfloat16)
    partial_terms = jnp.einsum(
        "rtc,cd->rtd", gated, out_projection, preferred_element_type=jnp.float32
    )
    return lax.psum_scatter(
        partial_terms.astype(jnp.bfloat16), "chan", scatter_dimension=2, tiled=True
    )


def rotate(block, axis, distance):
    n = lax.axis_size(axis)
    return lax.ppermute(block, axis, [(i, (i + distance) % n) for i in range(n)])


def exchange(block, axis, mask):
    return lax.ppermute(block, axis, [(i, i ^ mask) for i in range(lax.axis_size(axis))])


def vmem_call(kernel, outs, scratch, flops, *operands):
    moved = sum(x.size * x.dtype.itemsize for x in (*operands, *outs))
    return pl.pallas_call(
        kernel,
        out_shape=tuple(outs),
        in_specs=[pl.BlockSpec(memory_space=VMEM)] * len(operands),
        out_specs=tuple(pl.BlockSpec(memory_space=VMEM) for _ in outs),
        scratch_shapes=scratch,
        compiler_params=pltpu.CompilerParams(vmem_limit_bytes=40 * 1024 * 1024),
        cost_estimate=pl.CostEstimate(flops=flops, bytes_accessed=moved, transcendentals=0),
    )(*operands)


def pick_records(records, offsets):
    count = records.shape[0]

    def kernel(records_ref, out_ref, sems):
        z = lax.axis_index("seq")
        copies = [
            pltpu.make_async_copy(records_ref.at[lax.rem(z + k, count)], out_ref.at[i], sems.at[i])
            for i, k in enumerate(offsets)
        ]
        for copy in copies:
            copy.start()
        for copy in copies:
            copy.wait()

    return pl.pallas_call(
        kernel,
        out_shape=jax.ShapeDtypeStruct((len(offsets), *records.shape[1:]), records.dtype),
        in_specs=[pl.BlockSpec(memory_space=pl.ANY)],
        out_specs=pl.BlockSpec(memory_space=VMEM),
        scratch_shapes=[pltpu.SemaphoreType.DMA((len(offsets),))],
    )(records)


def pick_columns(out_projection):
    rows = out_projection.shape[0]

    def kernel(w_ref, one_ref, two_ref):
        me = lax.axis_index("chan")
        for mask, ref, start in ((1, one_ref, 0), (2, two_ref, 0), (3, two_ref, rows)):
            first = pl.multiple_of(jnp.bitwise_xor(me, mask) * LANES, LANES)
            ref[start : start + rows, :] = w_ref[:, pl.ds(first, LANES)]

    shape = lambda n: jax.ShapeDtypeStruct((n, LANES), out_projection.dtype)
    return vmem_call(kernel, [shape(rows), shape(2 * rows)], [], 0, out_projection)


def project(records, beside, across, diagonal, norm_gain, weights, short_kernel, taps, offsets):
    count, block_len, _ = records.shape
    picked = len(offsets)
    depth = weights.shape[1]
    f32, bf16 = jnp.float32, jnp.bfloat16

    def kernel(own_ref, beside_ref, across_ref, diagonal_ref, gain_ref, w_ref, short_ref, taps_ref, *rest):
        chunk_refs, (query_ref, w_all, shifted) = rest[:picked], rest[picked:]
        me = lax.axis_index("chan")
        z = lax.axis_index("seq")
        for j in range(4):
            first = pl.multiple_of(jnp.bitwise_xor(me, j) * LANES, LANES)
            for s in range(3):
                w_all[j * LANES : (j + 1) * LANES, s * LANES : (s + 1) * LANES] = w_ref[s, pl.ds(first, LANES), :]
        shifted[0:8, :] = jnp.zeros((8, 3 * LANES), f32)
        taps_block = taps_ref[...]
        flip = (
            lax.broadcasted_iota(jnp.int32, (LANES, LANES), 0)
            + lax.broadcasted_iota(jnp.int32, (LANES, LANES), 1)
            == LANES - 1
        ).astype(bf16)
        tap_rows = [
            jnp.dot(taps_block[:, b * LANES : (b + 1) * LANES], flip, preferred_element_type=f32)
            for b in range(block_len // LANES)
        ]
        for i, k in enumerate(offsets):
            rec = lax.rem(z + k, count)
            slabs = [own_ref[rec], beside_ref[rec], across_ref[i], diagonal_ref[i]]
            slabs = [s.astype(f32) for s in slabs]
            squares = slabs[0] * slabs[0]
            for s in slabs[1:]:
                squares = squares + s * s
            inv_rms = lax.rsqrt(jnp.sum(squares, axis=1, keepdims=True) * (1.0 / depth) + 1e-06)
            normed = [
                (s * inv_rms * gain_ref[pl.ds(jnp.bitwise_xor(me, j), 1), :]).astype(bf16)
                for j, s in enumerate(slabs)
            ]
            projected = jnp.dot(jnp.concatenate(normed, axis=1), w_all[...], preferred_element_type=f32)
            shifted[8:, :] = projected.astype(bf16).astype(f32)
            streams = []
            for s in range(3):
                cols = slice(s * LANES, (s + 1) * LANES)
                streams.append(
                    short_ref[0, s : s + 1, :] * shifted[8 : 8 + block_len, cols]
                    + short_ref[1, s : s + 1, :] * shifted[7 : 7 + block_len, cols]
                    + short_ref[2, s : s + 1, :] * shifted[6 : 6 + block_len, cols]
                )
            query_ref[i] = streams[0]
            chunk_refs[i][0:block_len, :] = (streams[1] * streams[2]).astype(bf16)
            heads = shifted[8:10, LANES:]
            tails = shifted[6 + block_len : 8 + block_len, :]
            rim = [heads[:, :LANES], heads[:, LANES:], tails[:, LANES : 2 * LANES], tails[:, 2 * LANES :], tails[:, :LANES]]
            extra = jnp.concatenate(tap_rows + rim + [jnp.zeros((EXTRA - 22, LANES), f32)], axis=0)
            chunk_refs[i][block_len:, :] = extra.astype(bf16)

    chunk = jax.ShapeDtypeStruct((block_len + EXTRA, LANES), bf16)
    query = jax.ShapeDtypeStruct((picked, block_len, LANES), f32)
    scratch = [pltpu.VMEM((4 * LANES, 3 * LANES), bf16), pltpu.VMEM((8 + block_len, 3 * LANES), f32)]
    out = vmem_call(
        kernel, [chunk] * picked + [query], scratch, 2 * picked * block_len * 512 * 384,
        records, beside, across, diagonal, norm_gain, weights, short_kernel, taps,
    )
    return out[:picked], out[picked]


def long_convolution(chunks, distances, short_kernel, skip_gain):
    n = len(chunks)
    block_len = chunks[0].shape[0] - EXTRA
    length = n * block_len
    pieces = block_len // LANES
    f32, bf16 = jnp.float32, jnp.bfloat16

    def kernel(*refs):
        chunk_refs, (short_ref, skip_ref), out_refs = refs[:n], refs[n : n + 2], refs[n + 2 : 2 * n + 2]
        inputs, source, bands, sums = refs[2 * n + 2 :]
        z = lax.axis_index("seq")
        for ref, k in zip(chunk_refs, distances):
            inputs[lax.rem(z - k + n, n)] = ref[...]
        lane = lax.broadcasted_iota(jnp.int32, (LANES, LANES), 1)
        tap_rows = [inputs[q, block_len : block_len + 4 * pieces, :].astype(f32) for q in range(n)]
        for f in range(4):
            row = [
                tap_rows[q][4 * b + f : 4 * b + f + 1, :] for q in reversed(range(n)) for b in reversed(range(pieces))
            ]
            row = jnp.concatenate(row + [jnp.zeros((1, LANES), f32)], axis=1)
            wide = jnp.broadcast_to(row, (LANES, length + LANES))
            band = pltpu.roll(wide, 1, 1, stride=1, stride_axis=0)
            bands[f * LANES : (f + 1) * LANES, :] = band.astype(bf16)
        short = [[short_ref[j, s : s + 1, :] for j in range(3)] for s in range(3)]
        for q in range(n):
            source[q * block_len : (q + 1) * block_len, :] = inputs[q, :block_len, :]
            if q == 0:
                continue
            here = inputs[q, block_len : block_len + EXTRA, :].astype(f32)[4 * pieces :]
            past = inputs[q - 1, block_len : block_len + EXTRA, :].astype(f32)[4 * pieces :]
            fixed = []
            for s in (1, 2):
                head, tail = here[2 * s - 2 : 2 * s], past[2 * s + 2 : 2 * s + 4]
                k0, k1, k2 = short[s]
                fixed.append(
                    (
                        k0 * head[0:1] + k1 * tail[1:2] + k2 * tail[0:1],
                        k0 * head[1:2] + k1 * head[0:1] + k2 * tail[1:2],
                    )
                )
            rows = [fixed[0][t] * fixed[1][t] for t in range(2)]
            first = source[q * block_len : q * block_len + 16, :].astype(f32)
            first = jnp.concatenate(rows + [first[2:]], axis=0)
            source[q * block_len : q * block_len + 16, :] = first.astype(bf16)
        for p in range(length // LANES):
            reach = (p + 1) * LANES
            terms = jnp.dot(bands[:, length + LANES - reach :], source[0:reach, :], preferred_element_type=f32)
            total = terms[0:LANES]
            for f in range(1, 4):
                total = jnp.where(lane >= f * 32, terms[f * LANES : (f + 1) * LANES], total)
            total = total + skip_ref[...] * source[reach - LANES : reach, :].astype(f32)
            q, b = divmod(p, pieces)
            sums[q, b * LANES : (b + 1) * LANES, :] = total.astype(bf16)
        for q in range(n):
            if q == 0:
                tail = jnp.zeros((2, LANES), f32)
            else:
                tail = inputs[q - 1, block_len : block_len + EXTRA, :].astype(f32)[20:22]
            sums[q, block_len:, :] = jnp.concatenate([tail, jnp.zeros((BACK - 2, LANES), f32)], axis=0).astype(bf16)
        for ref, k in zip(out_refs, distances):
            ref[...] = sums[lax.rem(z + k, n)]

    back = jax.ShapeDtypeStruct((block_len + BACK, LANES), bf16)
    scratch = [
        pltpu.VMEM((n, block_len + EXTRA, LANES), bf16),
        pltpu.VMEM((length, LANES), bf16),
        pltpu.VMEM((4 * LANES, length + LANES), bf16),
        pltpu.VMEM((n, block_len + BACK, LANES), bf16),
    ]
    return vmem_call(kernel, [back] * n, scratch, 4 * length * length * LANES, *chunks, short_kernel, skip_gain)


def gate(sums, queries, short_kernel):
    block_len = sums[0].shape[0] - BACK
    n = len(sums)
    f32, bf16 = jnp.float32, jnp.bfloat16
    arrays = []
    for array, _ in queries:
        if not any(array is a for a in arrays):
            arrays.append(array)
    places = [([a is array for a in arrays].index(True), index) for array, index in queries]

    def kernel(*refs):
        sum_refs, query_refs, short_ref, out_ref = refs[:n], refs[n:-2], refs[-2], refs[-1]
        for i, (a, index) in enumerate(places):
            tail = sum_refs[i][block_len:, :].astype(f32)
            k1, k2 = short_ref[1, 0:1, :], short_ref[2, 0:1, :]
            rim = [k1 * tail[1:2] + k2 * tail[0:1], k2 * tail[1:2], jnp.zeros((6, LANES), f32)]
            query = query_refs[a][index]
            query = jnp.concatenate([query[0:8] + jnp.concatenate(rim, axis=0), query[8:]], axis=0)
            out = query * sum_refs[i][0:block_len, :].astype(f32)
            out_ref[i * block_len : (i + 1) * block_len, :] = out.astype(bf16)

    out = jax.ShapeDtypeStruct((n * block_len, LANES), bf16)
    return vmem_call(kernel, [out], [], 0, *sums, *arrays, short_kernel)[0]


def mix(slabs, weights, distances, block_len):
    f32, bf16 = jnp.float32, jnp.bfloat16
    count = sum(len(d) for d in distances)
    groups = len(slabs)

    def kernel(*refs):
        slab_refs, (own_ref, beside_ref, far_ref, diagonal_ref) = refs[: 4 * groups], refs[4 * groups : 4 * groups + 4]
        out_ref, w_all = refs[-2:]
        me = lax.axis_index("chan")
        z = lax.axis_index("seq")
        w_all[0:LANES, :] = own_ref[:, pl.ds(pl.multiple_of(me * LANES, LANES), LANES)]
        w_all[LANES : 2 * LANES, :] = beside_ref[...]
        w_all[2 * LANES : 3 * LANES, :] = far_ref[0:LANES, :]
        w_all[3 * LANES :, :] = diagonal_ref[LANES:, :]
        for g in range(groups):
            for i, k in enumerate(distances[g]):
                rows = slice(i * block_len, (i + 1) * block_len)
                lhs = jnp.concatenate([ref[rows, :] for ref in slab_refs[4 * g : 4 * g + 4]], axis=1)
                out_ref[lax.rem(z + k, count)] = jnp.dot(lhs, w_all[...], preferred_element_type=f32).astype(bf16)

    out = jax.ShapeDtypeStruct((count, block_len, LANES), bf16)
    operands = [x for slab in slabs for x in slab] + list(weights)
    scratch = [pltpu.VMEM((4 * LANES, LANES), bf16)]
    return vmem_call(kernel, [out], scratch, 2 * count * block_len * 512 * LANES, *operands)[0]


def exchange_body(records, norm_gain, in_projection, short_kernel, long_filter, skip_gain, out_projection):
    block_len = records.shape[1]
    first = pick_records(records, (2, 1))
    across_first = exchange(first, "chan", 2)
    second = pick_records(records, (3, 0))
    across_second = exchange(second, "chan", 2)
    beside = exchange(records, "chan", 1)
    weights = jnp.transpose(in_projection, (1, 0, 2))
    gain = norm_gain.reshape(4, LANES)
    skip = skip_gain.reshape(1, LANES)

    diagonal_first = exchange(across_first, "chan", 1)
    (to_two, to_one), query_first = project(
        records, beside, across_first, diagonal_first, gain, weights, short_kernel, long_filter, (2, 1)
    )
    from_two = rotate(to_two, "seq", 2)
    from_one = rotate(to_one, "seq", 1)
    diagonal_second = exchange(across_second, "chan", 1)
    (to_three, kept), query_second = project(
        records, beside, across_second, diagonal_second, gain, weights, short_kernel, long_filter, (3, 0)
    )
    from_three = rotate(to_three, "seq", 3)

    w_beside, w_far = pick_columns(out_projection)
    w_beside = exchange(w_beside, "chan", 1)
    w_far = exchange(w_far, "chan", 2)
    w_diagonal = exchange(w_far, "chan", 1)

    back_two, back_one, back_three, back_own = long_convolution(
        (from_two, from_one, from_three, kept), (2, 1, 3, 0), short_kernel, skip
    )
    sums_two = rotate(back_two, "seq", 2)
    sums_one = rotate(back_one, "seq", 1)
    sums_three = rotate(back_three, "seq", 3)

    def share(gated):
        across = exchange(gated, "chan", 2)
        return (gated, exchange(gated, "chan", 1), across, exchange(across, "chan", 1))

    own = share(gate([back_own], [(query_second, 1)], short_kernel))
    near = share(gate([sums_one, sums_three], [(query_second, 0), (query_first, 1)], short_kernel))
    far = share(gate([sums_two], [(query_first, 0)], short_kernel))
    return mix(
        (own, near, far), (out_projection, w_beside, w_far, w_diagonal), ((0,), (3, 1), (2,)), block_len
    )


def solution(mesh):
    placed = (
        P("parts", "seq", "chan"),
        P(),
        P(None, None, "chan"),
        P(None, None, "chan"),
        P("chan", "seq"),
        P("chan"),
        P("chan", None),
    )

    def body(records, norm_gain, in_projection, short_kernel, long_filter, skip_gain, out_projection):
        count, block_len, channels = records.shape
        fits = (
            count == 4
            and mesh.shape["seq"] == count
            and mesh.shape["chan"] == 4
            and channels == LANES
            and block_len == 3 * LANES
            and long_filter.shape[0] == 4
        )
        chosen = exchange_body if fits else ring_body
        return chosen(records, norm_gain, in_projection, short_kernel, long_filter, skip_gain, out_projection)

    return jax.shard_map(
        body, mesh=mesh, in_specs=placed, out_specs=P("parts", "seq", "chan"), check_vma=False
    )
```

```python
import jax
import jax.numpy as jnp
from jax import lax
from jax.experimental import pallas as pl
from jax.experimental.pallas import tpu as pltpu
from jax.sharding import PartitionSpec as P

LANES = 128
EXTRA = 32
SPLIT = 2
SPACE = 1 << 30
FAR = 1 << 33
COST = pl.CostEstimate(flops=0, bytes_accessed=0, transcendentals=0)
BACK = 16
VMEM = pltpu.VMEM


def from_behind(block, axis, distance):
    devices = range(lax.axis_size(axis))
    route = [(i - distance, i) for i in devices if i - distance in devices]
    return lax.ppermute(block, axis, route)


def block_terms(taps_padded, offset, block_source, block_len):
    filter_count = taps_padded.shape[0]
    window = lax.dynamic_slice_in_dim(taps_padded, offset + 1, 2 * block_len - 1, 1)
    flipped = window[:, ::-1]
    padded = jnp.pad(flipped, ((0, 0), (0, 1)))
    tiled_taps = jnp.tile(padded, (1, block_len))
    toeplitz = tiled_taps[:, block_len - 1 : block_len - 1 + block_len * (2 * block_len - 1)]
    toeplitz = toeplitz.reshape(filter_count, block_len, 2 * block_len - 1)[:, :, :block_len]
    record_count = block_source.shape[0]
    grouped = block_source.reshape(record_count, block_len, filter_count, -1)
    return jnp.einsum("fab,rbfg->rafg", toeplitz, grouped, preferred_element_type=jnp.float32)


def ring_body(records, norm_gain, in_projection, short_kernel, long_filter, skip_gain, out_projection):
    gathered = lax.all_gather(records, "chan", axis=2, tiled=True)
    widened = gathered.astype(jnp.float32)
    inv_rms = lax.rsqrt(jnp.mean(widened * widened, axis=-1, keepdims=True) + 1e-06)
    normed = (widened * inv_rms * norm_gain).astype(jnp.bfloat16)
    projected = jnp.einsum(
        "rtd,dkc->rtkc", normed, in_projection, preferred_element_type=jnp.float32
    ).astype(jnp.bfloat16)
    rim_rows = from_behind(projected[:, -2:], "seq", 1)
    extended = jnp.concatenate([rim_rows, projected], axis=1).astype(jnp.float32)
    streams = (
        short_kernel[0] * extended[:, 2:]
        + short_kernel[1] * extended[:, 1:-1]
        + short_kernel[2] * extended[:, :-2]
    )
    query_gate = streams[:, :, 0]
    gated_source = (streams[:, :, 1] * streams[:, :, 2]).astype(jnp.bfloat16)
    record_count, block_len, channels = gated_source.shape
    all_taps = lax.all_gather(long_filter, "seq", axis=1, tiled=True)
    taps_padded = jnp.concatenate(
        [jnp.zeros((all_taps.shape[0], block_len), jnp.bfloat16), all_taps], axis=1
    )
    my_start = lax.axis_index("seq") * block_len
    cycle_stops = lax.axis_size("seq")
    long_sum = block_terms(taps_padded, 0, gated_source, block_len)

    def advance(stop_index, state):
        running_sum, visiting = state
        visiting = from_behind(visiting, "seq", 1)
        lag_start = stop_index * block_len
        running_sum = lax.cond(
            lag_start <= my_start,
            lambda running: running + block_terms(taps_padded, lag_start, visiting, block_len),
            lambda running: running,
            running_sum,
        )
        return (running_sum, visiting)

    long_sum, _ = lax.fori_loop(1, cycle_stops, advance, (long_sum, gated_source))
    long_out = long_sum.reshape(
        record_count, block_len, channels
    ) + skip_gain * gated_source.astype(jnp.float32)
    gated = (query_gate * long_out).astype(jnp.bfloat16)
    partial_terms = jnp.einsum(
        "rtc,cd->rtd", gated, out_projection, preferred_element_type=jnp.float32
    )
    return lax.psum_scatter(
        partial_terms.astype(jnp.bfloat16), "chan", scatter_dimension=2, tiled=True
    )


def rotate(block, axis, distance):
    n = lax.axis_size(axis)
    return lax.ppermute(block, axis, [(i, (i + distance) % n) for i in range(n)])


def exchange(block, axis, mask):
    return lax.ppermute(block, axis, [(i, i ^ mask) for i in range(lax.axis_size(axis))])


def vmem_call(kernel, outs, scratch, *operands, cost=0):
    return pl.pallas_call(
        kernel,
        out_shape=tuple(outs),
        in_specs=[pl.BlockSpec(memory_space=VMEM)] * len(operands),
        out_specs=tuple(pl.BlockSpec(memory_space=VMEM) for _ in outs),
        scratch_shapes=scratch,
        compiler_params=pltpu.CompilerParams(vmem_limit_bytes=40 * 1024 * 1024),
        cost_estimate=pl.CostEstimate(flops=cost, bytes_accessed=0, transcendentals=0),
    )(*operands)


def after(value, *done):
    return lax.optimization_barrier((value, *done))[0]


def pick(records, groups):
    count, block_len, _ = records.shape
    flat = [len(group) * block_len for group in groups]

    def kernel(records_ref, *rest):
        out_refs, sems = rest[:-1], rest[-1]
        z = lax.axis_index("seq")
        copies = []
        for ref, group in zip(out_refs, groups):
            for i, k in enumerate(group):
                place = ref.at[pl.ds(i * block_len, block_len)]
                copies.append(
                    pltpu.make_async_copy(records_ref.at[lax.rem(z + k, count)], place, sems.at[len(copies)])
                )
        for copy in copies:
            copy.start()
        for copy in copies:
            copy.wait()

    shapes = [VMEM((n, LANES), records.dtype) for n in flat]
    return pl.pallas_call(
        kernel,
        out_shape=tuple(shapes),
        in_specs=[pl.BlockSpec(memory_space=pl.ANY)],
        out_specs=tuple(pl.BlockSpec(memory_space=VMEM) for _ in shapes),
        scratch_shapes=[pltpu.SemaphoreType.DMA((count,))],
        cost_estimate=COST,
    )(records)


def project(own, beside, across, diagonal, norm_gain, weights, short_kernel, taps, offsets):
    count, block_len, _ = beside.shape
    picked = len(offsets)
    depth = weights.shape[1]
    f32, bf16 = jnp.float32, jnp.bfloat16

    def kernel(own_ref, beside_ref, across_ref, gain_ref, w_ref, short_ref, taps_ref, *rest):
        diagonal_refs, rest = rest[: len(diagonal)], rest[len(diagonal) :]
        chunk_refs, (query_ref, w_all, shifted) = rest[:picked], rest[picked:]
        per = len(diagonal) // picked
        me = lax.axis_index("chan")
        z = lax.axis_index("seq")
        for j in range(4):
            first = pl.multiple_of(jnp.bitwise_xor(me, j) * LANES, LANES)
            for s in range(3):
                w_all[j * LANES : (j + 1) * LANES, s * LANES : (s + 1) * LANES] = w_ref[s, pl.ds(first, LANES), :]
        shifted[0:8, :] = jnp.zeros((8, 3 * LANES), f32)
        taps_block = taps_ref[...]
        flip = (
            lax.broadcasted_iota(jnp.int32, (LANES, LANES), 0)
            + lax.broadcasted_iota(jnp.int32, (LANES, LANES), 1)
            == LANES - 1
        ).astype(bf16)
        tap_rows = [
            jnp.dot(taps_block[:, b * LANES : (b + 1) * LANES], flip, preferred_element_type=f32)
            for b in range(block_len // LANES)
        ]
        for i, k in enumerate(offsets):
            rec = lax.rem(z + k, count)
            rows = slice(i * block_len, (i + 1) * block_len)
            pieces = [ref[...] for ref in diagonal_refs[i * per : (i + 1) * per]]
            slabs = [own_ref[rows, :], beside_ref[rec], across_ref[rows, :], jnp.concatenate(pieces, axis=0)]
            slabs = [s.astype(f32) for s in slabs]
            squares = slabs[0] * slabs[0]
            for s in slabs[1:]:
                squares = squares + s * s
            inv_rms = lax.rsqrt(jnp.sum(squares, axis=1, keepdims=True) * (1.0 / depth) + 1e-06)
            normed = [
                (s * inv_rms * gain_ref[pl.ds(jnp.bitwise_xor(me, j), 1), :]).astype(bf16)
                for j, s in enumerate(slabs)
            ]
            projected = jnp.dot(jnp.concatenate(normed, axis=1), w_all[...], preferred_element_type=f32)
            shifted[8:, :] = projected.astype(bf16).astype(f32)
            streams = []
            for s in range(3):
                cols = slice(s * LANES, (s + 1) * LANES)
                streams.append(
                    short_ref[0, s : s + 1, :] * shifted[8 : 8 + block_len, cols]
                    + short_ref[1, s : s + 1, :] * shifted[7 : 7 + block_len, cols]
                    + short_ref[2, s : s + 1, :] * shifted[6 : 6 + block_len, cols]
                )
            query_ref[i] = streams[0]
            chunk_refs[i][0:block_len, :] = (streams[1] * streams[2]).astype(bf16)
            heads = shifted[8:10, LANES:]
            tails = shifted[6 + block_len : 8 + block_len, :]
            rim = [heads[:, :LANES], heads[:, LANES:], tails[:, LANES : 2 * LANES], tails[:, 2 * LANES :], tails[:, :LANES]]
            extra = jnp.concatenate(tap_rows + rim + [jnp.zeros((EXTRA - 22, LANES), f32)], axis=0)
            chunk_refs[i][block_len:, :] = extra.astype(bf16)

    chunk = jax.ShapeDtypeStruct((block_len + EXTRA, LANES), bf16)
    query = jax.ShapeDtypeStruct((picked, block_len, LANES), f32)
    scratch = [pltpu.VMEM((4 * LANES, 3 * LANES), bf16), pltpu.VMEM((8 + block_len, 3 * LANES), f32)]
    out = vmem_call(
        kernel, [chunk] * picked + [query], scratch,
        own, beside, across, norm_gain, weights, short_kernel, taps, *diagonal,
    )
    return out[:picked], out[picked]


def tail_rows(block, cost):
    def kernel(block_ref, out_ref):
        out_ref[...] = block_ref[-EXTRA:, :]

    return vmem_call(kernel, [jax.ShapeDtypeStruct((EXTRA, LANES), block.dtype)], [], block, cost=cost)[0]


def long_convolution(chunks, distances, first_tail, short_kernel, skip_gain):
    n = len(chunks)
    block_len = chunks[0].shape[0] - EXTRA
    length = n * block_len
    pieces = block_len // LANES
    f32, bf16 = jnp.float32, jnp.bfloat16

    def kernel(*refs):
        chunk_refs, (tail_ref, short_ref, skip_ref), out_refs = refs[:n], refs[n : n + 3], refs[n + 3 : 2 * n + 3]
        inputs, source, bands, sums = refs[2 * n + 3 :]
        z = lax.axis_index("seq")
        for ref, k in zip(chunk_refs, distances):
            inputs[lax.rem(z - k + n, n)] = ref[...]
        inputs[lax.rem(z - distances[0] + n, n), block_len:, :] = tail_ref[...]
        lane = lax.broadcasted_iota(jnp.int32, (LANES, LANES), 1)
        tap_rows = [inputs[q, block_len : block_len + 4 * pieces, :].astype(f32) for q in range(n)]
        for f in range(4):
            row = [
                tap_rows[q][4 * b + f : 4 * b + f + 1, :] for q in reversed(range(n)) for b in reversed(range(pieces))
            ]
            row = jnp.concatenate(row + [jnp.zeros((1, LANES), f32)], axis=1)
            wide = jnp.broadcast_to(row, (LANES, length + LANES))
            band = pltpu.roll(wide, 1, 1, stride=1, stride_axis=0)
            bands[f * LANES : (f + 1) * LANES, :] = band.astype(bf16)
        short = [[short_ref[j, s : s + 1, :] for j in range(3)] for s in range(3)]
        for q in range(n):
            source[q * block_len : (q + 1) * block_len, :] = inputs[q, :block_len, :]
            if q == 0:
                continue
            here = inputs[q, block_len : block_len + EXTRA, :].astype(f32)[4 * pieces :]
            past = inputs[q - 1, block_len : block_len + EXTRA, :].astype(f32)[4 * pieces :]
            fixed = []
            for s in (1, 2):
                head, tail = here[2 * s - 2 : 2 * s], past[2 * s + 2 : 2 * s + 4]
                k0, k1, k2 = short[s]
                fixed.append(
                    (
                        k0 * head[0:1] + k1 * tail[1:2] + k2 * tail[0:1],
                        k0 * head[1:2] + k1 * head[0:1] + k2 * tail[1:2],
                    )
                )
            rows = [fixed[0][t] * fixed[1][t] for t in range(2)]
            first = source[q * block_len : q * block_len + 16, :].astype(f32)
            first = jnp.concatenate(rows + [first[2:]], axis=0)
            source[q * block_len : q * block_len + 16, :] = first.astype(bf16)
        for p in range(length // LANES):
            reach = (p + 1) * LANES
            terms = jnp.dot(bands[:, length + LANES - reach :], source[0:reach, :], preferred_element_type=f32)
            total = terms[0:LANES]
            for f in range(1, 4):
                total = jnp.where(lane >= f * 32, terms[f * LANES : (f + 1) * LANES], total)
            total = total + skip_ref[...] * source[reach - LANES : reach, :].astype(f32)
            q, b = divmod(p, pieces)
            sums[q, b * LANES : (b + 1) * LANES, :] = total.astype(bf16)
        for q in range(n):
            if q == 0:
                tail = jnp.zeros((2, LANES), f32)
            else:
                tail = inputs[q - 1, block_len : block_len + EXTRA, :].astype(f32)[20:22]
            sums[q, block_len:, :] = jnp.concatenate([tail, jnp.zeros((BACK - 2, LANES), f32)], axis=0).astype(bf16)
        for ref, k in zip(out_refs, distances):
            ref[...] = sums[lax.rem(z + k, n)]

    back = jax.ShapeDtypeStruct((block_len + BACK, LANES), bf16)
    scratch = [
        pltpu.VMEM((n, block_len + EXTRA, LANES), bf16),
        pltpu.VMEM((length, LANES), bf16),
        pltpu.VMEM((4 * LANES, length + LANES), bf16),
        pltpu.VMEM((n, block_len + BACK, LANES), bf16),
    ]
    return vmem_call(kernel, [back] * n, scratch, *chunks, first_tail, short_kernel, skip_gain)


def gate(sums, queries, short_kernel, out_projection=None, cost=0):
    block_len = sums[0].shape[0] - BACK
    n = len(sums)
    f32, bf16 = jnp.float32, jnp.bfloat16
    arrays = []
    for array, _ in queries:
        if not any(array is a for a in arrays):
            arrays.append(array)
    places = [([a is array for a in arrays].index(True), index) for array, index in queries]

    masks = [()] if out_projection is None else [(2, 3), (1,)]

    def kernel(*refs):
        sum_refs, query_refs = refs[:n], refs[n : n + len(arrays)]
        short_ref, w_refs, out_refs = refs[n + len(arrays)], refs[n + len(arrays) + 1 : -len(masks)], refs[-len(masks) :]
        me = lax.axis_index("chan")
        for ref, targets in zip(out_refs, masks):
            for i, mask in enumerate(targets):
                first = pl.multiple_of(jnp.bitwise_xor(me, mask) * LANES, LANES)
                start = n * block_len + i * LANES
                ref[start : start + LANES, :] = w_refs[0][:, pl.ds(first, LANES)]
        for i, (a, index) in enumerate(places):
            tail = sum_refs[i][block_len:, :].astype(f32)
            k1, k2 = short_ref[1, 0:1, :], short_ref[2, 0:1, :]
            rim = [k1 * tail[1:2] + k2 * tail[0:1], k2 * tail[1:2], jnp.zeros((6, LANES), f32)]
            query = query_refs[a][index]
            query = jnp.concatenate([query[0:8] + jnp.concatenate(rim, axis=0), query[8:]], axis=0)
            out = query * sum_refs[i][0:block_len, :].astype(f32)
            for ref in out_refs:
                ref[i * block_len : (i + 1) * block_len, :] = out.astype(bf16)

    outs = [jax.ShapeDtypeStruct((n * block_len + len(m) * LANES, LANES), bf16) for m in masks]
    extra = [] if out_projection is None else [out_projection]
    return vmem_call(kernel, outs, [], *sums, *arrays, short_kernel, *extra, cost=cost)


def mix(slabs, out_projection, distances, block_len):
    f32, bf16 = jnp.float32, jnp.bfloat16
    count = sum(len(d) for d in distances)
    groups = len(slabs)

    def kernel(*refs):
        slab_refs, (w_ref, out_ref, w_all) = refs[: 4 * groups], refs[4 * groups :]
        me = lax.axis_index("chan")
        z = lax.axis_index("seq")
        start = len(distances[0]) * block_len
        w_all[0:LANES, :] = w_ref[:, pl.ds(pl.multiple_of(me * LANES, LANES), LANES)]
        w_all[LANES : 2 * LANES, :] = slab_refs[1][start : start + LANES, :]
        w_all[2 * LANES : 3 * LANES, :] = slab_refs[2][start : start + LANES, :]
        w_all[3 * LANES :, :] = slab_refs[3][start + LANES : start + 2 * LANES, :]
        for g in range(groups):
            for i, k in enumerate(distances[g]):
                rows = slice(i * block_len, (i + 1) * block_len)
                lhs = jnp.concatenate([ref[rows, :] for ref in slab_refs[4 * g : 4 * g + 4]], axis=1)
                out_ref[lax.rem(z + k, count)] = jnp.dot(lhs, w_all[...], preferred_element_type=f32).astype(bf16)

    out = jax.ShapeDtypeStruct((count, block_len, LANES), bf16)
    operands = [x for slab in slabs for x in slab] + [out_projection]
    return vmem_call(kernel, [out], [pltpu.VMEM((4 * LANES, LANES), bf16)], *operands)[0]


def exchange_body(records, norm_gain, in_projection, short_kernel, long_filter, skip_gain, out_projection):
    block_len = records.shape[1]
    weights = jnp.transpose(in_projection, (1, 0, 2))
    gain = norm_gain.reshape(4, LANES)
    skip = skip_gain.reshape(1, LANES)

    groups = ((2,), (1, 3, 0))
    picked = pick(records, groups)
    across = [exchange(block, "chan", 2) for block in picked]
    beside = exchange(records, "chan", 1)
    def projected(g, far):
        pieces = SPLIT * len(groups[g])
        size = far.shape[0] // pieces
        diagonal = [exchange(far[i * size : (i + 1) * size], "chan", 1) for i in range(pieces)]
        return project(
            picked[g], beside, far, diagonal, gain, weights, short_kernel, long_filter, groups[g]
        )

    (to_two,), query_two = projected(0, across[0])
    from_two = rotate(to_two, "seq", 2)
    (to_one, to_three, kept), query_rest = projected(1, after(across[1], to_two))
    from_one = rotate(to_one, "seq", 1)
    from_three = rotate(to_three, "seq", 3)

    back_two, back_one, back_three, back_own = long_convolution(
        (from_two, from_one, from_three, kept),
        (2, 1, 3, 0),
        tail_rows(from_two, SPACE),
        short_kernel,
        skip,
    )
    sums_two = rotate(back_two, "seq", 2)
    sums_one = rotate(back_one, "seq", 1)
    sums_three = rotate(back_three, "seq", 3)

    own, own_beside = gate([back_own], [(query_rest, 2)], short_kernel, out_projection)
    own_over = exchange(own, "chan", 2)
    (near,) = gate([after(sums_one, own), after(sums_three, own)], [(query_rest, 1), (query_rest, 0)], short_kernel)
    (far,) = gate([after(sums_two, near, own_over)], [(query_two, 0)], short_kernel, cost=FAR)
    slabs = []
    for gated, beside, over in ((own, own_beside, own_over), (near, near, None), (far, far, None)):
        if over is None:
            over = exchange(gated, "chan", 2)
        slabs.append((gated, exchange(beside, "chan", 1), over, exchange(after(over, far), "chan", 1)))
    return mix(slabs, out_projection, ((0,), (3, 1), (2,)), block_len)


def solution(mesh):
    placed = (
        P("parts", "seq", "chan"),
        P(),
        P(None, None, "chan"),
        P(None, None, "chan"),
        P("chan", "seq"),
        P("chan"),
        P("chan", None),
    )

    def body(records, norm_gain, in_projection, short_kernel, long_filter, skip_gain, out_projection):
        count, block_len, channels = records.shape
        fits = (
            count == 4
            and mesh.shape["seq"] == count
            and mesh.shape["chan"] == 4
            and channels == LANES
            and block_len == 3 * LANES
            and long_filter.shape[0] == 4
        )
        chosen = exchange_body if fits else ring_body
        return chosen(records, norm_gain, in_projection, short_kernel, long_filter, skip_gain, out_projection)

    return jax.shard_map(
        body, mesh=mesh, in_specs=placed, out_specs=P("parts", "seq", "chan"), check_vma=False
    )
```

```python
import jax
import jax.numpy as jnp
from jax import lax
from jax.experimental import pallas as pl
from jax.experimental.pallas import tpu as pltpu
from jax.sharding import PartitionSpec as P

LANES = 128
EXTRA = 32
SPLIT = 1
SPACE = 1 << 31
FAR = 1 << 32
NEAR = (1, 3)
TIE = 1
FARD = (2,)
ORDER = (2, 1, 3)
BESIDE = 1
OWNSEP = 1
SPLIT1 = 2
COST = pl.CostEstimate(flops=0, bytes_accessed=0, transcendentals=0)
BACK = 16
VMEM = pltpu.VMEM


def from_behind(block, axis, distance):
    devices = range(lax.axis_size(axis))
    route = [(i - distance, i) for i in devices if i - distance in devices]
    return lax.ppermute(block, axis, route)


def block_terms(taps_padded, offset, block_source, block_len):
    filter_count = taps_padded.shape[0]
    window = lax.dynamic_slice_in_dim(taps_padded, offset + 1, 2 * block_len - 1, 1)
    flipped = window[:, ::-1]
    padded = jnp.pad(flipped, ((0, 0), (0, 1)))
    tiled_taps = jnp.tile(padded, (1, block_len))
    toeplitz = tiled_taps[:, block_len - 1 : block_len - 1 + block_len * (2 * block_len - 1)]
    toeplitz = toeplitz.reshape(filter_count, block_len, 2 * block_len - 1)[:, :, :block_len]
    record_count = block_source.shape[0]
    grouped = block_source.reshape(record_count, block_len, filter_count, -1)
    return jnp.einsum("fab,rbfg->rafg", toeplitz, grouped, preferred_element_type=jnp.float32)


def ring_body(records, norm_gain, in_projection, short_kernel, long_filter, skip_gain, out_projection):
    gathered = lax.all_gather(records, "chan", axis=2, tiled=True)
    widened = gathered.astype(jnp.float32)
    inv_rms = lax.rsqrt(jnp.mean(widened * widened, axis=-1, keepdims=True) + 1e-06)
    normed = (widened * inv_rms * norm_gain).astype(jnp.bfloat16)
    projected = jnp.einsum(
        "rtd,dkc->rtkc", normed, in_projection, preferred_element_type=jnp.float32
    ).astype(jnp.bfloat16)
    rim_rows = from_behind(projected[:, -2:], "seq", 1)
    extended = jnp.concatenate([rim_rows, projected], axis=1).astype(jnp.float32)
    streams = (
        short_kernel[0] * extended[:, 2:]
        + short_kernel[1] * extended[:, 1:-1]
        + short_kernel[2] * extended[:, :-2]
    )
    query_gate = streams[:, :, 0]
    gated_source = (streams[:, :, 1] * streams[:, :, 2]).astype(jnp.bfloat16)
    record_count, block_len, channels = gated_source.shape
    all_taps = lax.all_gather(long_filter, "seq", axis=1, tiled=True)
    taps_padded = jnp.concatenate(
        [jnp.zeros((all_taps.shape[0], block_len), jnp.bfloat16), all_taps], axis=1
    )
    my_start = lax.axis_index("seq") * block_len
    cycle_stops = lax.axis_size("seq")
    long_sum = block_terms(taps_padded, 0, gated_source, block_len)

    def advance(stop_index, state):
        running_sum, visiting = state
        visiting = from_behind(visiting, "seq", 1)
        lag_start = stop_index * block_len
        running_sum = lax.cond(
            lag_start <= my_start,
            lambda running: running + block_terms(taps_padded, lag_start, visiting, block_len),
            lambda running: running,
            running_sum,
        )
        return (running_sum, visiting)

    long_sum, _ = lax.fori_loop(1, cycle_stops, advance, (long_sum, gated_source))
    long_out = long_sum.reshape(
        record_count, block_len, channels
    ) + skip_gain * gated_source.astype(jnp.float32)
    gated = (query_gate * long_out).astype(jnp.bfloat16)
    partial_terms = jnp.einsum(
        "rtc,cd->rtd", gated, out_projection, preferred_element_type=jnp.float32
    )
    return lax.psum_scatter(
        partial_terms.astype(jnp.bfloat16), "chan", scatter_dimension=2, tiled=True
    )


def rotate(block, axis, distance):
    n = lax.axis_size(axis)
    return lax.ppermute(block, axis, [(i, (i + distance) % n) for i in range(n)])


def exchange(block, axis, mask):
    return lax.ppermute(block, axis, [(i, i ^ mask) for i in range(lax.axis_size(axis))])


def vmem_call(kernel, outs, scratch, *operands, cost=0):
    return pl.pallas_call(
        kernel,
        out_shape=tuple(outs),
        in_specs=[pl.BlockSpec(memory_space=VMEM)] * len(operands),
        out_specs=tuple(pl.BlockSpec(memory_space=VMEM) for _ in outs),
        scratch_shapes=scratch,
        compiler_params=pltpu.CompilerParams(vmem_limit_bytes=40 * 1024 * 1024),
        cost_estimate=pl.CostEstimate(flops=cost, bytes_accessed=0, transcendentals=0),
    )(*operands)


def after(value, *done):
    return lax.optimization_barrier((value, *done))[0]


def pick(records, groups):
    count, block_len, _ = records.shape
    flat = [len(group) * block_len for group in groups]

    def kernel(records_ref, *rest):
        out_refs, sems = rest[:-1], rest[-1]
        z = lax.axis_index("seq")
        copies = []
        for ref, group in zip(out_refs, groups):
            for i, k in enumerate(group):
                place = ref.at[pl.ds(i * block_len, block_len)]
                copies.append(
                    pltpu.make_async_copy(records_ref.at[lax.rem(z + k, count)], place, sems.at[len(copies)])
                )
        for copy in copies:
            copy.start()
        for copy in copies:
            copy.wait()

    shapes = [VMEM((n, LANES), records.dtype) for n in flat]
    return pl.pallas_call(
        kernel,
        out_shape=tuple(shapes),
        in_specs=[pl.BlockSpec(memory_space=pl.ANY)],
        out_specs=tuple(pl.BlockSpec(memory_space=VMEM) for _ in shapes),
        scratch_shapes=[pltpu.SemaphoreType.DMA((count,))],
        cost_estimate=COST,
    )(records)


def project(own, beside, across, diagonal, norm_gain, weights, short_kernel, taps, offsets):
    count, block_len, _ = beside.shape
    picked = len(offsets)
    depth = weights.shape[1]
    f32, bf16 = jnp.float32, jnp.bfloat16

    def kernel(own_ref, beside_ref, across_ref, gain_ref, w_ref, short_ref, taps_ref, *rest):
        diagonal_refs, rest = rest[: len(diagonal)], rest[len(diagonal) :]
        chunk_refs, (query_ref, w_all, shifted) = rest[:picked], rest[picked:]
        per = len(diagonal) // picked
        me = lax.axis_index("chan")
        z = lax.axis_index("seq")
        for j in range(4):
            first = pl.multiple_of(jnp.bitwise_xor(me, j) * LANES, LANES)
            for s in range(3):
                w_all[j * LANES : (j + 1) * LANES, s * LANES : (s + 1) * LANES] = w_ref[s, pl.ds(first, LANES), :]
        shifted[0:8, :] = jnp.zeros((8, 3 * LANES), f32)
        taps_block = taps_ref[...]
        flip = (
            lax.broadcasted_iota(jnp.int32, (LANES, LANES), 0)
            + lax.broadcasted_iota(jnp.int32, (LANES, LANES), 1)
            == LANES - 1
        ).astype(bf16)
        tap_rows = [
            jnp.dot(taps_block[:, b * LANES : (b + 1) * LANES], flip, preferred_element_type=f32)
            for b in range(block_len // LANES)
        ]
        for i, k in enumerate(offsets):
            rec = lax.rem(z + k, count)
            rows = slice(i * block_len, (i + 1) * block_len)
            pieces = [ref[...] for ref in diagonal_refs[i * per : (i + 1) * per]]
            slabs = [own_ref[rows, :], beside_ref[rec], across_ref[rows, :], jnp.concatenate(pieces, axis=0)]
            slabs = [s.astype(f32) for s in slabs]
            squares = slabs[0] * slabs[0]
            for s in slabs[1:]:
                squares = squares + s * s
            inv_rms = lax.rsqrt(jnp.sum(squares, axis=1, keepdims=True) * (1.0 / depth) + 1e-06)
            normed = [
                (s * inv_rms * gain_ref[pl.ds(jnp.bitwise_xor(me, j), 1), :]).astype(bf16)
                for j, s in enumerate(slabs)
            ]
            projected = jnp.dot(jnp.concatenate(normed, axis=1), w_all[...], preferred_element_type=f32)
            shifted[8:, :] = projected.astype(bf16).astype(f32)
            streams = []
            for s in range(3):
                cols = slice(s * LANES, (s + 1) * LANES)
                streams.append(
                    short_ref[0, s : s + 1, :] * shifted[8 : 8 + block_len, cols]
                    + short_ref[1, s : s + 1, :] * shifted[7 : 7 + block_len, cols]
                    + short_ref[2, s : s + 1, :] * shifted[6 : 6 + block_len, cols]
                )
            query_ref[i] = streams[0]
            chunk_refs[i][0:block_len, :] = (streams[1] * streams[2]).astype(bf16)
            heads = shifted[8:10, LANES:]
            tails = shifted[6 + block_len : 8 + block_len, :]
            rim = [heads[:, :LANES], heads[:, LANES:], tails[:, LANES : 2 * LANES], tails[:, 2 * LANES :], tails[:, :LANES]]
            extra = jnp.concatenate(tap_rows + rim + [jnp.zeros((EXTRA - 22, LANES), f32)], axis=0)
            chunk_refs[i][block_len:, :] = extra.astype(bf16)

    chunk = jax.ShapeDtypeStruct((block_len + EXTRA, LANES), bf16)
    query = jax.ShapeDtypeStruct((picked, block_len, LANES), f32)
    scratch = [pltpu.VMEM((4 * LANES, 3 * LANES), bf16), pltpu.VMEM((8 + block_len, 3 * LANES), f32)]
    out = vmem_call(
        kernel, [chunk] * picked + [query], scratch,
        own, beside, across, norm_gain, weights, short_kernel, taps, *diagonal,
    )
    return out[:picked], out[picked]


def tail_rows(block, skip_gain, cost):
    def kernel(block_ref, skip_ref, out_ref, same_ref):
        out_ref[...] = block_ref[-EXTRA:, :]
        same_ref[...] = skip_ref[...]

    outs = [jax.ShapeDtypeStruct((EXTRA, LANES), block.dtype), jax.ShapeDtypeStruct(skip_gain.shape, skip_gain.dtype)]
    return vmem_call(kernel, outs, [], block, skip_gain, cost=cost)


def long_convolution(chunks, distances, first_tail, short_kernel, skip_gain):
    n = len(chunks)
    block_len = chunks[0].shape[0] - EXTRA
    length = n * block_len
    half = length // 2
    pieces = block_len // LANES
    f32, bf16 = jnp.float32, jnp.bfloat16

    def kernel(*refs):
        chunk_refs, (tail_ref, short_ref, skip_ref), out_refs = refs[:n], refs[n : n + 3], refs[n + 3 : 2 * n + 3]
        inputs, source, bands, sums = refs[2 * n + 3 :]
        z = lax.axis_index("seq")
        for ref, k in zip(chunk_refs, distances):
            inputs[lax.rem(z - k + n, n)] = ref[...]
        inputs[lax.rem(z - distances[0] + n, n), block_len:, :] = tail_ref[...]
        lane = lax.broadcasted_iota(jnp.int32, (LANES, LANES), 1)
        tap_rows = [inputs[q, block_len : block_len + 4 * pieces, :].astype(f32) for q in range(n)]
        for f in range(4):
            row = [
                tap_rows[q][4 * b + f : 4 * b + f + 1, :] for q in reversed(range(n)) for b in reversed(range(pieces))
            ]
            row = jnp.concatenate(row + [jnp.zeros((1, LANES), f32)], axis=1)
            wide = jnp.broadcast_to(row, (LANES, length + LANES))
            band = pltpu.roll(wide, 1, 1, stride=1, stride_axis=0)
            bands[f * LANES : (f + 1) * LANES, :] = band.astype(bf16)
        short = [[short_ref[j, s : s + 1, :] for j in range(3)] for s in range(3)]
        for q in range(n):
            side, start = divmod(q * block_len, half)
            columns = slice(side * LANES, (side + 1) * LANES)
            source[start : start + block_len, columns] = inputs[q, :block_len, :]
            if q == 0:
                continue
            here = inputs[q, block_len : block_len + EXTRA, :].astype(f32)[4 * pieces :]
            past = inputs[q - 1, block_len : block_len + EXTRA, :].astype(f32)[4 * pieces :]
            fixed = []
            for s in (1, 2):
                head, tail = here[2 * s - 2 : 2 * s], past[2 * s + 2 : 2 * s + 4]
                k0, k1, k2 = short[s]
                fixed.append(
                    (
                        k0 * head[0:1] + k1 * tail[1:2] + k2 * tail[0:1],
                        k0 * head[1:2] + k1 * head[0:1] + k2 * tail[1:2],
                    )
                )
            first = inputs[q, 0:16, :].astype(f32)
            first = jnp.concatenate([fixed[0][t] * fixed[1][t] for t in range(2)] + [first[2:]], axis=0)
            source[start : start + 16, columns] = first.astype(bf16)

        def finish(p, terms):
            side, start = divmod(p * LANES, half)
            total = terms[0:LANES]
            for f in range(1, 4):
                total = jnp.where(lane >= f * 32, terms[f * LANES : (f + 1) * LANES], total)
            here = source[start : start + LANES, side * LANES : (side + 1) * LANES]
            total = total + skip_ref[...] * here.astype(f32)
            q, b = divmod(p, pieces)
            sums[q, b * LANES : (b + 1) * LANES, :] = total.astype(bf16)

        width = length + LANES
        for p in range(half // LANES):
            reach = (p + 1) * LANES
            within = jnp.dot(bands[:, width - reach :], source[0:reach, :], preferred_element_type=f32)
            across = jnp.dot(
                bands[:, width - reach - half : width - reach], source[:, 0:LANES], preferred_element_type=f32
            )
            finish(p, within[:, 0:LANES])
            finish(p + half // LANES, within[:, LANES:] + across)
        for q in range(n):
            if q == 0:
                tail = jnp.zeros((2, LANES), f32)
            else:
                tail = inputs[q - 1, block_len : block_len + EXTRA, :].astype(f32)[20:22]
            sums[q, block_len:, :] = jnp.concatenate([tail, jnp.zeros((BACK - 2, LANES), f32)], axis=0).astype(bf16)
        for ref, k in zip(out_refs, distances):
            ref[...] = sums[lax.rem(z + k, n)]

    back = jax.ShapeDtypeStruct((block_len + BACK, LANES), bf16)
    scratch = [
        pltpu.VMEM((n, block_len + EXTRA, LANES), bf16),
        pltpu.VMEM((half, 2 * LANES), bf16),
        pltpu.VMEM((4 * LANES, length + LANES), bf16),
        pltpu.VMEM((n, block_len + BACK, LANES), bf16),
    ]
    return vmem_call(kernel, [back] * n, scratch, *chunks, first_tail, short_kernel, skip_gain)


def gate(sums, queries, short_kernel, out_projection=None, cost=0):
    block_len = sums[0].shape[0] - BACK
    n = len(sums)
    f32, bf16 = jnp.float32, jnp.bfloat16
    arrays = []
    for array, _ in queries:
        if not any(array is a for a in arrays):
            arrays.append(array)
    places = [([a is array for a in arrays].index(True), index) for array, index in queries]

    masks = [()] if out_projection is None else [(2, 3), (1,)]

    def kernel(*refs):
        sum_refs, query_refs = refs[:n], refs[n : n + len(arrays)]
        short_ref, w_refs, out_refs = refs[n + len(arrays)], refs[n + len(arrays) + 1 : -len(masks)], refs[-len(masks) :]
        me = lax.axis_index("chan")
        for ref, targets in zip(out_refs, masks):
            for i, mask in enumerate(targets):
                first = pl.multiple_of(jnp.bitwise_xor(me, mask) * LANES, LANES)
                start = n * block_len + i * LANES
                ref[start : start + LANES, :] = w_refs[0][:, pl.ds(first, LANES)]
        for i, (a, index) in enumerate(places):
            tail = sum_refs[i][block_len:, :].astype(f32)
            k1, k2 = short_ref[1, 0:1, :], short_ref[2, 0:1, :]
            rim = [k1 * tail[1:2] + k2 * tail[0:1], k2 * tail[1:2], jnp.zeros((6, LANES), f32)]
            query = query_refs[a][index]
            query = jnp.concatenate([query[0:8] + jnp.concatenate(rim, axis=0), query[8:]], axis=0)
            out = query * sum_refs[i][0:block_len, :].astype(f32)
            for ref in out_refs:
                ref[i * block_len : (i + 1) * block_len, :] = out.astype(bf16)

    outs = [jax.ShapeDtypeStruct((n * block_len + len(m) * LANES, LANES), bf16) for m in masks]
    extra = [] if out_projection is None else [out_projection]
    return vmem_call(kernel, outs, [], *sums, *arrays, short_kernel, *extra, cost=cost)


def mix(slabs, out_projection, distances, block_len):
    f32, bf16 = jnp.float32, jnp.bfloat16
    count = sum(len(d) for d in distances)
    groups = len(slabs)

    def kernel(*refs):
        slab_refs, (w_ref, out_ref, w_all, mixed, sems) = refs[: 4 * groups], refs[4 * groups :]
        copies = []
        me = lax.axis_index("chan")
        z = lax.axis_index("seq")
        start = len(distances[0]) * block_len
        w_all[0:LANES, :] = w_ref[:, pl.ds(pl.multiple_of(me * LANES, LANES), LANES)]
        w_all[LANES : 2 * LANES, :] = slab_refs[1][start : start + LANES, :]
        w_all[2 * LANES : 3 * LANES, :] = slab_refs[2][start : start + LANES, :]
        w_all[3 * LANES :, :] = slab_refs[3][start + LANES : start + 2 * LANES, :]
        for g in range(groups):
            for i, k in enumerate(distances[g]):
                rows = slice(i * block_len, (i + 1) * block_len)
                lhs = jnp.concatenate([ref[rows, :] for ref in slab_refs[4 * g : 4 * g + 4]], axis=1)
                n = len(copies)
                mixed[n] = jnp.dot(lhs, w_all[...], preferred_element_type=f32).astype(bf16)
                copies.append(pltpu.make_async_copy(mixed.at[n], out_ref.at[lax.rem(z + k, count)], sems.at[n]))
                copies[n].start()
        for copy in copies:
            copy.wait()

    operands = [x for slab in slabs for x in slab] + [out_projection]
    return pl.pallas_call(
        kernel,
        out_shape=jax.ShapeDtypeStruct((count, block_len, LANES), bf16),
        in_specs=[pl.BlockSpec(memory_space=VMEM)] * len(operands),
        out_specs=pl.BlockSpec(memory_space=pl.ANY),
        scratch_shapes=[
            pltpu.VMEM((4 * LANES, LANES), bf16),
            pltpu.VMEM((count, block_len, LANES), bf16),
            pltpu.SemaphoreType.DMA((count,)),
        ],
        compiler_params=pltpu.CompilerParams(vmem_limit_bytes=40 * 1024 * 1024),
        cost_estimate=COST,
    )(*operands)


def exchange_body(records, norm_gain, in_projection, short_kernel, long_filter, skip_gain, out_projection):
    block_len = records.shape[1]
    weights = jnp.transpose(in_projection, (1, 0, 2))
    gain = norm_gain.reshape(4, LANES)
    skip = skip_gain.reshape(1, LANES)

    groups = ((2,), (1, 3, 0))
    picked = pick(records, groups)
    across = [exchange(block, "chan", 2) for block in picked]
    beside = exchange(after(records, picked[0]) if BESIDE else records, "chan", 1)

    def projected(offsets, own, far, pieces):
        size = far.shape[0] // pieces
        diagonal = [exchange(far[i * size : (i + 1) * size], "chan", 1) for i in range(pieces)]
        return project(own, beside, far, diagonal, gain, weights, short_kernel, long_filter, offsets)

    query = {}
    (to_two,), query_two = projected((2,), picked[0], across[0], SPLIT1)
    from_two = rotate(to_two, "seq", 2)
    second = after(across[1], to_two)
    if OWNSEP:
        rows = 2 * block_len
        (to_one, to_three), query_near = projected((1, 3), picked[1][:rows], second[:rows], 2 * SPLIT)
        last = after(second[rows:], to_one)
        (kept,), query_own = projected((0,), picked[1][rows:], last, 1)
        query = {0: (query_own, 0), 1: (query_near, 1), 3: (query_near, 0), 2: (query_two, 0)}
    else:
        (to_one, to_three, kept), query_rest = projected((1, 3, 0), picked[1], second, 3 * SPLIT)
        query = {0: (query_rest, 2), 1: (query_rest, 1), 3: (query_rest, 0), 2: (query_two, 0)}
    from_one = rotate(to_one, "seq", 1)
    from_three = rotate(to_three, "seq", 3)

    tail, skip = tail_rows(from_two, skip, SPACE)
    back_two, back_one, back_three, back_own = long_convolution(
        (from_two, from_one, from_three, kept), (2, 1, 3, 0), tail, short_kernel, skip
    )
    back = {1: back_one, 2: back_two, 3: back_three}
    sums = {k: rotate(back[k], "seq", k) for k in ORDER}

    own, own_beside = gate([back_own], [query[0]], short_kernel, out_projection)
    own_over = exchange(own, "chan", 2)
    (near,) = gate([after(sums[k], own) for k in NEAR], [query[k] for k in NEAR], short_kernel)
    (far,) = gate([after(sums[k], near, own_over) if TIE == 0 else after(sums[k], near) for k in FARD], [query[k] for k in FARD], short_kernel, cost=FAR)
    if TIE == 1:
        far = after(far, own_over)
    slabs = []
    for gated, beside, over in ((own, own_beside, own_over), (near, near, None), (far, far, None)):
        if over is None:
            over = exchange(gated, "chan", 2)
        slabs.append((gated, exchange(beside, "chan", 1), over, exchange(after(over, far), "chan", 1)))
    places = [tuple((4 - k) % 4 for k in group) for group in ((0,), NEAR, FARD)]
    return mix(slabs, out_projection, places, block_len)


def solution(mesh):
    placed = (
        P("parts", "seq", "chan"),
        P(),
        P(None, None, "chan"),
        P(None, None, "chan"),
        P("chan", "seq"),
        P("chan"),
        P("chan", None),
    )

    def body(records, norm_gain, in_projection, short_kernel, long_filter, skip_gain, out_projection):
        count, block_len, channels = records.shape
        fits = (
            count == 4
            and mesh.shape["seq"] == count
            and mesh.shape["chan"] == 4
            and channels == LANES
            and block_len == 3 * LANES
            and long_filter.shape[0] == 4
        )
        chosen = exchange_body if fits else ring_body
        return chosen(records, norm_gain, in_projection, short_kernel, long_filter, skip_gain, out_projection)

    return jax.shard_map(
        body, mesh=mesh, in_specs=placed, out_specs=P("parts", "seq", "chan"), check_vma=False
    )
```

```python
import jax
import jax.numpy as jnp
from jax import lax
from jax.experimental import pallas as pl
from jax.experimental.pallas import tpu as pltpu
from jax.sharding import PartitionSpec as P

LANES = 128
EXTRA = 32
NO_COST = pl.CostEstimate(flops=0, bytes_accessed=0, transcendentals=0)
EARLY_COST, FAR_COST = 1 << 30, 1 << 33
BACK = 16
VMEM = pltpu.VMEM


def from_behind(block, axis, distance):
    devices = range(lax.axis_size(axis))
    route = [(i - distance, i) for i in devices if i - distance in devices]
    return lax.ppermute(block, axis, route)


def block_terms(taps_padded, offset, block_source, block_len):
    filter_count = taps_padded.shape[0]
    window = lax.dynamic_slice_in_dim(taps_padded, offset + 1, 2 * block_len - 1, 1)
    flipped = window[:, ::-1]
    padded = jnp.pad(flipped, ((0, 0), (0, 1)))
    tiled_taps = jnp.tile(padded, (1, block_len))
    toeplitz = tiled_taps[:, block_len - 1 : block_len - 1 + block_len * (2 * block_len - 1)]
    toeplitz = toeplitz.reshape(filter_count, block_len, 2 * block_len - 1)[:, :, :block_len]
    record_count = block_source.shape[0]
    grouped = block_source.reshape(record_count, block_len, filter_count, -1)
    return jnp.einsum("fab,rbfg->rafg", toeplitz, grouped, preferred_element_type=jnp.float32)


def ring_body(records, norm_gain, in_projection, short_kernel, long_filter, skip_gain, out_projection):
    gathered = lax.all_gather(records, "chan", axis=2, tiled=True)
    widened = gathered.astype(jnp.float32)
    inv_rms = lax.rsqrt(jnp.mean(widened * widened, axis=-1, keepdims=True) + 1e-06)
    normed = (widened * inv_rms * norm_gain).astype(jnp.bfloat16)
    projected = jnp.einsum(
        "rtd,dkc->rtkc", normed, in_projection, preferred_element_type=jnp.float32
    ).astype(jnp.bfloat16)
    rim_rows = from_behind(projected[:, -2:], "seq", 1)
    extended = jnp.concatenate([rim_rows, projected], axis=1).astype(jnp.float32)
    streams = (
        short_kernel[0] * extended[:, 2:]
        + short_kernel[1] * extended[:, 1:-1]
        + short_kernel[2] * extended[:, :-2]
    )
    query_gate = streams[:, :, 0]
    gated_source = (streams[:, :, 1] * streams[:, :, 2]).astype(jnp.bfloat16)
    record_count, block_len, channels = gated_source.shape
    all_taps = lax.all_gather(long_filter, "seq", axis=1, tiled=True)
    taps_padded = jnp.concatenate(
        [jnp.zeros((all_taps.shape[0], block_len), jnp.bfloat16), all_taps], axis=1
    )
    my_start = lax.axis_index("seq") * block_len
    cycle_stops = lax.axis_size("seq")
    long_sum = block_terms(taps_padded, 0, gated_source, block_len)

    def advance(stop_index, state):
        running_sum, visiting = state
        visiting = from_behind(visiting, "seq", 1)
        lag_start = stop_index * block_len
        running_sum = lax.cond(
            lag_start <= my_start,
            lambda running: running + block_terms(taps_padded, lag_start, visiting, block_len),
            lambda running: running,
            running_sum,
        )
        return (running_sum, visiting)

    long_sum, _ = lax.fori_loop(1, cycle_stops, advance, (long_sum, gated_source))
    long_out = long_sum.reshape(
        record_count, block_len, channels
    ) + skip_gain * gated_source.astype(jnp.float32)
    gated = (query_gate * long_out).astype(jnp.bfloat16)
    partial_terms = jnp.einsum(
        "rtc,cd->rtd", gated, out_projection, preferred_element_type=jnp.float32
    )
    return lax.psum_scatter(
        partial_terms.astype(jnp.bfloat16), "chan", scatter_dimension=2, tiled=True
    )


def rotate(block, axis, distance):
    n = lax.axis_size(axis)
    return lax.ppermute(block, axis, [(i, (i + distance) % n) for i in range(n)])


def exchange(block, axis, mask):
    return lax.ppermute(block, axis, [(i, i ^ mask) for i in range(lax.axis_size(axis))])


def vmem_call(kernel, outs, scratch, *operands, cost=0):
    return pl.pallas_call(
        kernel,
        out_shape=tuple(outs),
        in_specs=[pl.BlockSpec(memory_space=VMEM)] * len(operands),
        out_specs=tuple(pl.BlockSpec(memory_space=VMEM) for _ in outs),
        scratch_shapes=scratch,
        compiler_params=pltpu.CompilerParams(vmem_limit_bytes=40 * 1024 * 1024),
        cost_estimate=pl.CostEstimate(flops=cost, bytes_accessed=0, transcendentals=0),
    )(*operands)


def after(value, *done):
    return lax.optimization_barrier((value, *done))[0]


def pick(records, groups):
    count, block_len, _ = records.shape
    flat = [len(group) * block_len for group in groups]

    def kernel(records_ref, *rest):
        out_refs, sems = rest[:-1], rest[-1]
        z = lax.axis_index("seq")
        copies = []
        for ref, group in zip(out_refs, groups):
            for i, k in enumerate(group):
                place = ref.at[pl.ds(i * block_len, block_len)]
                copies.append(
                    pltpu.make_async_copy(records_ref.at[lax.rem(z + k, count)], place, sems.at[len(copies)])
                )
        for copy in copies:
            copy.start()
        for copy in copies:
            copy.wait()

    shapes = [VMEM((n, LANES), records.dtype) for n in flat]
    return pl.pallas_call(
        kernel,
        out_shape=tuple(shapes),
        in_specs=[pl.BlockSpec(memory_space=pl.ANY)],
        out_specs=tuple(pl.BlockSpec(memory_space=VMEM) for _ in shapes),
        scratch_shapes=[pltpu.SemaphoreType.DMA((count,))],
        cost_estimate=NO_COST,
    )(records)


def project(own, beside, across, diagonal, norm_gain, weights, short_kernel, taps, offsets):
    count, block_len, _ = beside.shape
    picked = len(offsets)
    depth = weights.shape[1]
    f32, bf16 = jnp.float32, jnp.bfloat16

    def kernel(own_ref, beside_ref, across_ref, gain_ref, w_ref, short_ref, taps_ref, *rest):
        diagonal_refs, rest = rest[: len(diagonal)], rest[len(diagonal) :]
        chunk_refs, (query_ref, w_all, shifted) = rest[:picked], rest[picked:]
        per = len(diagonal) // picked
        me = lax.axis_index("chan")
        z = lax.axis_index("seq")
        for j in range(4):
            first = pl.multiple_of(jnp.bitwise_xor(me, j) * LANES, LANES)
            for s in range(3):
                w_all[j * LANES : (j + 1) * LANES, s * LANES : (s + 1) * LANES] = w_ref[s, pl.ds(first, LANES), :]
        shifted[0:8, :] = jnp.zeros((8, 3 * LANES), f32)
        taps_block = taps_ref[...]
        flip = (
            lax.broadcasted_iota(jnp.int32, (LANES, LANES), 0)
            + lax.broadcasted_iota(jnp.int32, (LANES, LANES), 1)
            == LANES - 1
        ).astype(bf16)
        tap_rows = [
            jnp.dot(taps_block[:, b * LANES : (b + 1) * LANES], flip, preferred_element_type=f32)
            for b in range(block_len // LANES)
        ]
        for i, k in enumerate(offsets):
            rec = lax.rem(z + k, count)
            rows = slice(i * block_len, (i + 1) * block_len)
            pieces = [ref[...] for ref in diagonal_refs[i * per : (i + 1) * per]]
            slabs = [own_ref[rows, :], beside_ref[rec], across_ref[rows, :], jnp.concatenate(pieces, axis=0)]
            slabs = [s.astype(f32) for s in slabs]
            squares = slabs[0] * slabs[0]
            for s in slabs[1:]:
                squares = squares + s * s
            inv_rms = lax.rsqrt(jnp.sum(squares, axis=1, keepdims=True) * (1.0 / depth) + 1e-06)
            normed = [
                (s * inv_rms * gain_ref[pl.ds(jnp.bitwise_xor(me, j), 1), :]).astype(bf16)
                for j, s in enumerate(slabs)
            ]
            projected = jnp.dot(jnp.concatenate(normed, axis=1), w_all[...], preferred_element_type=f32)
            shifted[8:, :] = projected.astype(bf16).astype(f32)
            streams = []
            for s in range(3):
                cols = slice(s * LANES, (s + 1) * LANES)
                streams.append(
                    short_ref[0, s : s + 1, :] * shifted[8 : 8 + block_len, cols]
                    + short_ref[1, s : s + 1, :] * shifted[7 : 7 + block_len, cols]
                    + short_ref[2, s : s + 1, :] * shifted[6 : 6 + block_len, cols]
                )
            query_ref[i] = streams[0]
            chunk_refs[i][0:block_len, :] = (streams[1] * streams[2]).astype(bf16)
            heads = shifted[8:10, LANES:]
            tails = shifted[6 + block_len : 8 + block_len, :]
            rim = [heads[:, :LANES], heads[:, LANES:], tails[:, LANES : 2 * LANES], tails[:, 2 * LANES :], tails[:, :LANES]]
            extra = jnp.concatenate(tap_rows + rim + [jnp.zeros((EXTRA - 22, LANES), f32)], axis=0)
            chunk_refs[i][block_len:, :] = extra.astype(bf16)

    chunk = jax.ShapeDtypeStruct((block_len + EXTRA, LANES), bf16)
    query = jax.ShapeDtypeStruct((picked, block_len, LANES), f32)
    scratch = [pltpu.VMEM((4 * LANES, 3 * LANES), bf16), pltpu.VMEM((8 + block_len, 3 * LANES), f32)]
    out = vmem_call(
        kernel, [chunk] * picked + [query], scratch,
        own, beside, across, norm_gain, weights, short_kernel, taps, *diagonal,
    )
    return out[:picked], out[picked]


def tail_rows(block, skip_gain, cost):
    def kernel(block_ref, skip_ref, out_ref, same_ref):
        out_ref[...] = block_ref[-EXTRA:, :]
        same_ref[...] = skip_ref[...]

    outs = [jax.ShapeDtypeStruct((EXTRA, LANES), block.dtype), jax.ShapeDtypeStruct(skip_gain.shape, skip_gain.dtype)]
    return vmem_call(kernel, outs, [], block, skip_gain, cost=cost)


def long_convolution(chunks, distances, first_tail, short_kernel, skip_gain):
    n = len(chunks)
    block_len = chunks[0].shape[0] - EXTRA
    length = n * block_len
    half = length // 2
    pieces = block_len // LANES
    f32, bf16 = jnp.float32, jnp.bfloat16

    def kernel(*refs):
        chunk_refs, (tail_ref, short_ref, skip_ref), out_refs = refs[:n], refs[n : n + 3], refs[n + 3 : 2 * n + 3]
        inputs, source, bands, sums = refs[2 * n + 3 :]
        z = lax.axis_index("seq")
        for ref, k in zip(chunk_refs, distances):
            inputs[lax.rem(z - k + n, n)] = ref[...]
        inputs[lax.rem(z - distances[0] + n, n), block_len:, :] = tail_ref[...]
        lane = lax.broadcasted_iota(jnp.int32, (LANES, LANES), 1)
        tap_rows = [inputs[q, block_len : block_len + 4 * pieces, :].astype(f32) for q in range(n)]
        for f in range(4):
            row = [
                tap_rows[q][4 * b + f : 4 * b + f + 1, :] for q in reversed(range(n)) for b in reversed(range(pieces))
            ]
            row = jnp.concatenate(row + [jnp.zeros((1, LANES), f32)], axis=1)
            wide = jnp.broadcast_to(row, (LANES, length + LANES))
            band = pltpu.roll(wide, 1, 1, stride=1, stride_axis=0)
            bands[f * LANES : (f + 1) * LANES, :] = band.astype(bf16)
        short = [[short_ref[j, s : s + 1, :] for j in range(3)] for s in range(3)]
        for q in range(n):
            side, start = divmod(q * block_len, half)
            columns = slice(side * LANES, (side + 1) * LANES)
            source[start : start + block_len, columns] = inputs[q, :block_len, :]
            if q == 0:
                continue
            here = inputs[q, block_len : block_len + EXTRA, :].astype(f32)[4 * pieces :]
            past = inputs[q - 1, block_len : block_len + EXTRA, :].astype(f32)[4 * pieces :]
            fixed = []
            for s in (1, 2):
                head, tail = here[2 * s - 2 : 2 * s], past[2 * s + 2 : 2 * s + 4]
                k0, k1, k2 = short[s]
                fixed.append(
                    (
                        k0 * head[0:1] + k1 * tail[1:2] + k2 * tail[0:1],
                        k0 * head[1:2] + k1 * head[0:1] + k2 * tail[1:2],
                    )
                )
            first = inputs[q, 0:16, :].astype(f32)
            first = jnp.concatenate([fixed[0][t] * fixed[1][t] for t in range(2)] + [first[2:]], axis=0)
            source[start : start + 16, columns] = first.astype(bf16)

        def finish(p, terms):
            side, start = divmod(p * LANES, half)
            total = terms[0:LANES]
            for f in range(1, 4):
                total = jnp.where(lane >= f * 32, terms[f * LANES : (f + 1) * LANES], total)
            here = source[start : start + LANES, side * LANES : (side + 1) * LANES]
            total = total + skip_ref[...] * here.astype(f32)
            q, b = divmod(p, pieces)
            sums[q, b * LANES : (b + 1) * LANES, :] = total.astype(bf16)

        width = length + LANES
        for p in range(half // LANES):
            reach = (p + 1) * LANES
            within = jnp.dot(bands[:, width - reach :], source[0:reach, :], preferred_element_type=f32)
            across = jnp.dot(
                bands[:, width - reach - half : width - reach], source[:, 0:LANES], preferred_element_type=f32
            )
            finish(p, within[:, 0:LANES])
            finish(p + half // LANES, within[:, LANES:] + across)
        for q in range(n):
            if q == 0:
                tail = jnp.zeros((2, LANES), f32)
            else:
                tail = inputs[q - 1, block_len : block_len + EXTRA, :].astype(f32)[20:22]
            sums[q, block_len:, :] = jnp.concatenate([tail, jnp.zeros((BACK - 2, LANES), f32)], axis=0).astype(bf16)
        for ref, k in zip(out_refs, distances):
            ref[...] = sums[lax.rem(z + k, n)]

    back = jax.ShapeDtypeStruct((block_len + BACK, LANES), bf16)
    scratch = [
        pltpu.VMEM((n, block_len + EXTRA, LANES), bf16),
        pltpu.VMEM((half, 2 * LANES), bf16),
        pltpu.VMEM((4 * LANES, length + LANES), bf16),
        pltpu.VMEM((n, block_len + BACK, LANES), bf16),
    ]
    return vmem_call(kernel, [back] * n, scratch, *chunks, first_tail, short_kernel, skip_gain)


def gate(sums, queries, short_kernel, out_projection=None, cost=0):
    block_len = sums[0].shape[0] - BACK
    n = len(sums)
    f32, bf16 = jnp.float32, jnp.bfloat16
    arrays = []
    for array, _ in queries:
        if not any(array is a for a in arrays):
            arrays.append(array)
    places = [([a is array for a in arrays].index(True), index) for array, index in queries]

    masks = [()] if out_projection is None else [(2, 3), (1,)]

    def kernel(*refs):
        sum_refs, query_refs = refs[:n], refs[n : n + len(arrays)]
        short_ref, w_refs, out_refs = refs[n + len(arrays)], refs[n + len(arrays) + 1 : -len(masks)], refs[-len(masks) :]
        me = lax.axis_index("chan")
        for ref, targets in zip(out_refs, masks):
            for i, mask in enumerate(targets):
                first = pl.multiple_of(jnp.bitwise_xor(me, mask) * LANES, LANES)
                start = n * block_len + i * LANES
                ref[start : start + LANES, :] = w_refs[0][:, pl.ds(first, LANES)]
        for i, (a, index) in enumerate(places):
            tail = sum_refs[i][block_len:, :].astype(f32)
            k1, k2 = short_ref[1, 0:1, :], short_ref[2, 0:1, :]
            rim = [k1 * tail[1:2] + k2 * tail[0:1], k2 * tail[1:2], jnp.zeros((6, LANES), f32)]
            query = query_refs[a][index]
            query = jnp.concatenate([query[0:8] + jnp.concatenate(rim, axis=0), query[8:]], axis=0)
            out = query * sum_refs[i][0:block_len, :].astype(f32)
            for ref in out_refs:
                ref[i * block_len : (i + 1) * block_len, :] = out.astype(bf16)

    outs = [jax.ShapeDtypeStruct((n * block_len + len(m) * LANES, LANES), bf16) for m in masks]
    extra = [] if out_projection is None else [out_projection]
    return vmem_call(kernel, outs, [], *sums, *arrays, short_kernel, *extra, cost=cost)


def mix(slabs, out_projection, distances, shape, mixed=None):
    f32, bf16 = jnp.float32, jnp.bfloat16
    count, block_len, _ = shape
    groups = len(slabs)
    records = sum(len(d) for d in distances)
    first = mixed is None

    def kernel(*refs):
        slab_refs, w_ref, rest = refs[: 4 * groups], refs[4 * groups], refs[4 * groups + 1 :]
        if first:
            out_ref, w_all, results, sems = rest
            me = lax.axis_index("chan")
            start = len(distances[0]) * block_len
            w_all[0:LANES, :] = w_ref[:, pl.ds(pl.multiple_of(me * LANES, LANES), LANES)]
            w_all[LANES : 2 * LANES, :] = slab_refs[1][start : start + LANES, :]
            w_all[2 * LANES : 3 * LANES, :] = slab_refs[2][start : start + LANES, :]
            w_all[3 * LANES :, :] = slab_refs[3][start + LANES : start + 2 * LANES, :]
        else:
            w_all, (_, out_ref, results, sems) = w_ref, rest
        z = lax.axis_index("seq")
        copies = []
        for g in range(groups):
            for i, k in enumerate(distances[g]):
                rows = slice(i * block_len, (i + 1) * block_len)
                lhs = jnp.concatenate([ref[rows, :] for ref in slab_refs[4 * g : 4 * g + 4]], axis=1)
                n = len(copies)
                results[n] = jnp.dot(lhs, w_all[...], preferred_element_type=f32).astype(bf16)
                copies.append(pltpu.make_async_copy(results.at[n], out_ref.at[lax.rem(z + k, count)], sems.at[n]))
                copies[n].start()
        for copy in copies:
            copy.wait()

    whole, anywhere = pl.BlockSpec(memory_space=VMEM), pl.BlockSpec(memory_space=pl.ANY)
    operands = [x for slab in slabs for x in slab] + [out_projection]
    out_shape, out_specs = [jax.ShapeDtypeStruct(shape, bf16)], [anywhere]
    if first:
        out_shape.append(VMEM((4 * LANES, LANES), bf16))
        out_specs.append(whole)
    return pl.pallas_call(
        kernel,
        out_shape=tuple(out_shape),
        in_specs=[whole] * len(operands) + ([] if first else [anywhere]),
        out_specs=tuple(out_specs),
        input_output_aliases={} if first else {len(operands): 0},
        scratch_shapes=[pltpu.VMEM((records, block_len, LANES), bf16), pltpu.SemaphoreType.DMA((records,))],
        compiler_params=pltpu.CompilerParams(vmem_limit_bytes=40 * 1024 * 1024),
        cost_estimate=NO_COST,
    )(*operands, *([] if first else [mixed]))


def exchange_body(records, norm_gain, in_projection, short_kernel, long_filter, skip_gain, out_projection):
    weights = jnp.transpose(in_projection, (1, 0, 2))
    gain = norm_gain.reshape(4, LANES)
    skip = skip_gain.reshape(1, LANES)

    (first,) = pick(records, ((2,),))
    second, third = pick(records, ((1, 3), (0,)))
    across_first, across_second, across_third = (exchange(block, "chan", 2) for block in (first, second, third))
    beside = exchange(after(records, first), "chan", 1)

    def projected(offsets, own, far, pieces):
        size = far.shape[0] // pieces
        diagonal = [exchange(far[i * size : (i + 1) * size], "chan", 1) for i in range(pieces)]
        return project(own, beside, far, diagonal, gain, weights, short_kernel, long_filter, offsets)

    (to_two,), query_two = projected((2,), first, across_first, 2)
    from_two = rotate(to_two, "seq", 2)
    (to_one, to_three), query_near = projected((1, 3), second, after(across_second, to_two), 2)
    from_one = rotate(to_one, "seq", 1)
    from_three = rotate(to_three, "seq", 3)
    (kept,), query_own = projected((0,), third, after(across_third, to_one), 1)

    tail, skip = tail_rows(from_two, skip, EARLY_COST)
    back_two, back_one, back_three, back_own = long_convolution(
        (from_two, from_one, from_three, kept), (2, 1, 3, 0), tail, short_kernel, skip
    )
    sums_two = rotate(back_two, "seq", 2)
    sums_one = rotate(back_one, "seq", 1)
    sums_three = rotate(back_three, "seq", 3)

    own, own_beside = gate([back_own], [(query_own, 0)], short_kernel, out_projection)
    own_over = exchange(own, "chan", 2)
    (near,) = gate([after(sums_one, own), after(sums_three, own)], [(query_near, 1), (query_near, 0)], short_kernel)
    near_over = exchange(near, "chan", 2)
    (far,) = gate([after(sums_two, near)], [(query_two, 0)], short_kernel, cost=FAR_COST)
    far = after(far, own_over)
    far_over = exchange(far, "chan", 2)

    def slab(gated, beside, over):
        return (gated, exchange(beside, "chan", 1), over, exchange(after(over, far), "chan", 1))

    early = [slab(own, own_beside, own_over), slab(near, near, near_over)]
    mixed, columns = mix(early, out_projection, ((0,), (3, 1)), records.shape)
    return mix([slab(far, far, far_over)], columns, ((2,),), records.shape, mixed)[0]


def solution(mesh):
    placed = (
        P("parts", "seq", "chan"),
        P(),
        P(None, None, "chan"),
        P(None, None, "chan"),
        P("chan", "seq"),
        P("chan"),
        P("chan", None),
    )

    def body(records, norm_gain, in_projection, short_kernel, long_filter, skip_gain, out_projection):
        count, block_len, channels = records.shape
        fits = (
            count == 4
            and mesh.shape["seq"] == count
            and mesh.shape["chan"] == 4
            and channels == LANES
            and block_len == 3 * LANES
            and long_filter.shape[0] == 4
        )
        chosen = exchange_body if fits else ring_body
        return chosen(records, norm_gain, in_projection, short_kernel, long_filter, skip_gain, out_projection)

    return jax.shard_map(
        body, mesh=mesh, in_specs=placed, out_specs=P("parts", "seq", "chan"), check_vma=False
    )
```

```python
import jax
import jax.numpy as jnp
from jax import lax
from jax.experimental import pallas as pl
from jax.experimental.pallas import tpu as pltpu
from jax.sharding import PartitionSpec as P

LANES = 128
EXTRA = 32
NO_COST = pl.CostEstimate(flops=0, bytes_accessed=0, transcendentals=0)
EARLY_COST, FAR_COST = 1 << 30, 1 << 33
GRANT = 40 * 1024 * 1024
BACK = 16
VMEM = pltpu.VMEM


def from_behind(block, axis, distance):
    devices = range(lax.axis_size(axis))
    route = [(i - distance, i) for i in devices if i - distance in devices]
    return lax.ppermute(block, axis, route)


def block_terms(taps_padded, offset, block_source, block_len):
    filter_count = taps_padded.shape[0]
    window = lax.dynamic_slice_in_dim(taps_padded, offset + 1, 2 * block_len - 1, 1)
    flipped = window[:, ::-1]
    padded = jnp.pad(flipped, ((0, 0), (0, 1)))
    tiled_taps = jnp.tile(padded, (1, block_len))
    toeplitz = tiled_taps[:, block_len - 1 : block_len - 1 + block_len * (2 * block_len - 1)]
    toeplitz = toeplitz.reshape(filter_count, block_len, 2 * block_len - 1)[:, :, :block_len]
    record_count = block_source.shape[0]
    grouped = block_source.reshape(record_count, block_len, filter_count, -1)
    return jnp.einsum("fab,rbfg->rafg", toeplitz, grouped, preferred_element_type=jnp.float32)


def ring_body(records, norm_gain, in_projection, short_kernel, long_filter, skip_gain, out_projection):
    gathered = lax.all_gather(records, "chan", axis=2, tiled=True)
    widened = gathered.astype(jnp.float32)
    inv_rms = lax.rsqrt(jnp.mean(widened * widened, axis=-1, keepdims=True) + 1e-06)
    normed = (widened * inv_rms * norm_gain).astype(jnp.bfloat16)
    projected = jnp.einsum(
        "rtd,dkc->rtkc", normed, in_projection, preferred_element_type=jnp.float32
    ).astype(jnp.bfloat16)
    rim_rows = from_behind(projected[:, -2:], "seq", 1)
    extended = jnp.concatenate([rim_rows, projected], axis=1).astype(jnp.float32)
    streams = (
        short_kernel[0] * extended[:, 2:]
        + short_kernel[1] * extended[:, 1:-1]
        + short_kernel[2] * extended[:, :-2]
    )
    query_gate = streams[:, :, 0]
    gated_source = (streams[:, :, 1] * streams[:, :, 2]).astype(jnp.bfloat16)
    record_count, block_len, channels = gated_source.shape
    all_taps = lax.all_gather(long_filter, "seq", axis=1, tiled=True)
    taps_padded = jnp.concatenate(
        [jnp.zeros((all_taps.shape[0], block_len), jnp.bfloat16), all_taps], axis=1
    )
    my_start = lax.axis_index("seq") * block_len
    cycle_stops = lax.axis_size("seq")
    long_sum = block_terms(taps_padded, 0, gated_source, block_len)

    def advance(stop_index, state):
        running_sum, visiting = state
        visiting = from_behind(visiting, "seq", 1)
        lag_start = stop_index * block_len
        running_sum = lax.cond(
            lag_start <= my_start,
            lambda running: running + block_terms(taps_padded, lag_start, visiting, block_len),
            lambda running: running,
            running_sum,
        )
        return (running_sum, visiting)

    long_sum, _ = lax.fori_loop(1, cycle_stops, advance, (long_sum, gated_source))
    long_out = long_sum.reshape(
        record_count, block_len, channels
    ) + skip_gain * gated_source.astype(jnp.float32)
    gated = (query_gate * long_out).astype(jnp.bfloat16)
    partial_terms = jnp.einsum(
        "rtc,cd->rtd", gated, out_projection, preferred_element_type=jnp.float32
    )
    return lax.psum_scatter(
        partial_terms.astype(jnp.bfloat16), "chan", scatter_dimension=2, tiled=True
    )


def rotate(block, axis, distance):
    n = lax.axis_size(axis)
    return lax.ppermute(block, axis, [(i, (i + distance) % n) for i in range(n)])


def exchange(block, axis, mask):
    return lax.ppermute(block, axis, [(i, i ^ mask) for i in range(lax.axis_size(axis))])


def vmem_call(kernel, outs, scratch, *operands, cost=0):
    return pl.pallas_call(
        kernel,
        out_shape=tuple(outs),
        in_specs=[pl.BlockSpec(memory_space=VMEM)] * len(operands),
        out_specs=tuple(pl.BlockSpec(memory_space=VMEM) for _ in outs),
        scratch_shapes=scratch,
        compiler_params=pltpu.CompilerParams(vmem_limit_bytes=GRANT),
        cost_estimate=pl.CostEstimate(flops=cost, bytes_accessed=0, transcendentals=0),
    )(*operands)


def after(value, *done):
    return lax.optimization_barrier((value, *done))[0]


def pick(records, groups):
    count, block_len, _ = records.shape
    flat = [len(group) * block_len for group in groups]

    def kernel(records_ref, *rest):
        out_refs, sems = rest[:-1], rest[-1]
        z = lax.axis_index("seq")
        copies = []
        for ref, group in zip(out_refs, groups):
            for i, k in enumerate(group):
                place = ref.at[pl.ds(i * block_len, block_len)]
                copies.append(
                    pltpu.make_async_copy(records_ref.at[lax.rem(z + k, count)], place, sems.at[len(copies)])
                )
        for copy in copies:
            copy.start()
        for copy in copies:
            copy.wait()

    shapes = [VMEM((n, LANES), records.dtype) for n in flat]
    return pl.pallas_call(
        kernel,
        out_shape=tuple(shapes),
        in_specs=[pl.BlockSpec(memory_space=pl.ANY)],
        out_specs=tuple(pl.BlockSpec(memory_space=VMEM) for _ in shapes),
        scratch_shapes=[pltpu.SemaphoreType.DMA((count,))],
        cost_estimate=NO_COST,
    )(records)


def project(own, beside, across, diagonal, norm_gain, weights, short_kernel, taps, offsets):
    count, block_len, _ = beside.shape
    picked = len(offsets)
    depth = weights.shape[1]
    f32, bf16 = jnp.float32, jnp.bfloat16

    def kernel(own_ref, beside_ref, across_ref, gain_ref, w_ref, short_ref, taps_ref, *rest):
        diagonal_refs, rest = rest[: len(diagonal)], rest[len(diagonal) :]
        chunk_refs, (query_ref, w_all, shifted) = rest[:picked], rest[picked:]
        per = len(diagonal) // picked
        me = lax.axis_index("chan")
        z = lax.axis_index("seq")
        for j in range(4):
            first = pl.multiple_of(jnp.bitwise_xor(me, j) * LANES, LANES)
            for s in range(3):
                w_all[j * LANES : (j + 1) * LANES, s * LANES : (s + 1) * LANES] = w_ref[s, pl.ds(first, LANES), :]
        shifted[0:8, :] = jnp.zeros((8, 3 * LANES), f32)
        taps_block = taps_ref[...]
        flip = (
            lax.broadcasted_iota(jnp.int32, (LANES, LANES), 0)
            + lax.broadcasted_iota(jnp.int32, (LANES, LANES), 1)
            == LANES - 1
        ).astype(bf16)
        tap_rows = [
            jnp.dot(taps_block[:, b * LANES : (b + 1) * LANES], flip, preferred_element_type=f32)
            for b in range(block_len // LANES)
        ]
        for i, k in enumerate(offsets):
            rec = lax.rem(z + k, count)
            rows = slice(i * block_len, (i + 1) * block_len)
            pieces = [ref[...] for ref in diagonal_refs[i * per : (i + 1) * per]]
            slabs = [own_ref[rows, :], beside_ref[rec], across_ref[rows, :], jnp.concatenate(pieces, axis=0)]
            slabs = [s.astype(f32) for s in slabs]
            squares = slabs[0] * slabs[0]
            for s in slabs[1:]:
                squares = squares + s * s
            inv_rms = lax.rsqrt(jnp.sum(squares, axis=1, keepdims=True) * (1.0 / depth) + 1e-06)
            normed = [
                (s * inv_rms * gain_ref[pl.ds(jnp.bitwise_xor(me, j), 1), :]).astype(bf16)
                for j, s in enumerate(slabs)
            ]
            projected = jnp.dot(jnp.concatenate(normed, axis=1), w_all[...], preferred_element_type=f32)
            shifted[8:, :] = projected.astype(bf16).astype(f32)
            streams = []
            for s in range(3):
                cols = slice(s * LANES, (s + 1) * LANES)
                streams.append(
                    short_ref[0, s : s + 1, :] * shifted[8 : 8 + block_len, cols]
                    + short_ref[1, s : s + 1, :] * shifted[7 : 7 + block_len, cols]
                    + short_ref[2, s : s + 1, :] * shifted[6 : 6 + block_len, cols]
                )
            query_ref[i] = streams[0]
            chunk_refs[i][0:block_len, :] = (streams[1] * streams[2]).astype(bf16)
            heads = shifted[8:10, LANES:]
            tails = shifted[6 + block_len : 8 + block_len, :]
            rim = [heads[:, :LANES], heads[:, LANES:], tails[:, LANES : 2 * LANES], tails[:, 2 * LANES :], tails[:, :LANES]]
            extra = jnp.concatenate(tap_rows + rim + [jnp.zeros((EXTRA - 22, LANES), f32)], axis=0)
            chunk_refs[i][block_len:, :] = extra.astype(bf16)

    chunk = jax.ShapeDtypeStruct((block_len + EXTRA, LANES), bf16)
    query = jax.ShapeDtypeStruct((picked, block_len, LANES), f32)
    scratch = [pltpu.VMEM((4 * LANES, 3 * LANES), bf16), pltpu.VMEM((8 + block_len, 3 * LANES), f32)]
    out = vmem_call(
        kernel, [chunk] * picked + [query], scratch,
        own, beside, across, norm_gain, weights, short_kernel, taps, *diagonal,
    )
    return out[:picked], out[picked]


def tail_rows(block, skip_gain, cost):
    def kernel(block_ref, skip_ref, out_ref, same_ref):
        out_ref[...] = block_ref[-EXTRA:, :]
        same_ref[...] = skip_ref[...]

    outs = [jax.ShapeDtypeStruct((EXTRA, LANES), block.dtype), jax.ShapeDtypeStruct(skip_gain.shape, skip_gain.dtype)]
    return vmem_call(kernel, outs, [], block, skip_gain, cost=cost)


def long_convolution(chunks, distances, first_tail, short_kernel, skip_gain):
    n = len(chunks)
    block_len = chunks[0].shape[0] - EXTRA
    length = n * block_len
    half = length // 2
    pieces = block_len // LANES
    f32, bf16 = jnp.float32, jnp.bfloat16

    def kernel(*refs):
        chunk_refs, (tail_ref, short_ref, skip_ref), out_refs = refs[:n], refs[n : n + 3], refs[n + 3 : 2 * n + 3]
        inputs, source, bands, sums = refs[2 * n + 3 :]
        z = lax.axis_index("seq")
        for ref, k in zip(chunk_refs, distances):
            inputs[lax.rem(z - k + n, n)] = ref[...]
        inputs[lax.rem(z - distances[0] + n, n), block_len:, :] = tail_ref[...]
        lane = lax.broadcasted_iota(jnp.int32, (LANES, LANES), 1)
        tap_rows = [inputs[q, block_len : block_len + 4 * pieces, :].astype(f32) for q in range(n)]
        for f in range(4):
            row = [
                tap_rows[q][4 * b + f : 4 * b + f + 1, :] for q in reversed(range(n)) for b in reversed(range(pieces))
            ]
            row = jnp.concatenate(row + [jnp.zeros((1, LANES), f32)], axis=1)
            wide = jnp.broadcast_to(row, (LANES, length + LANES))
            band = pltpu.roll(wide, 1, 1, stride=1, stride_axis=0)
            bands[f * LANES : (f + 1) * LANES, :] = band.astype(bf16)
        short = [[short_ref[j, s : s + 1, :] for j in range(3)] for s in range(3)]
        for q in range(n):
            side, start = divmod(q * block_len, half)
            columns = slice(side * LANES, (side + 1) * LANES)
            source[start : start + block_len, columns] = inputs[q, :block_len, :]
            if q == 0:
                continue
            here = inputs[q, block_len : block_len + EXTRA, :].astype(f32)[4 * pieces :]
            past = inputs[q - 1, block_len : block_len + EXTRA, :].astype(f32)[4 * pieces :]
            fixed = []
            for s in (1, 2):
                head, tail = here[2 * s - 2 : 2 * s], past[2 * s + 2 : 2 * s + 4]
                k0, k1, k2 = short[s]
                fixed.append(
                    (
                        k0 * head[0:1] + k1 * tail[1:2] + k2 * tail[0:1],
                        k0 * head[1:2] + k1 * head[0:1] + k2 * tail[1:2],
                    )
                )
            first = inputs[q, 0:16, :].astype(f32)
            first = jnp.concatenate([fixed[0][t] * fixed[1][t] for t in range(2)] + [first[2:]], axis=0)
            source[start : start + 16, columns] = first.astype(bf16)

        def finish(p, terms):
            side, start = divmod(p * LANES, half)
            total = terms[0:LANES]
            for f in range(1, 4):
                total = jnp.where(lane >= f * 32, terms[f * LANES : (f + 1) * LANES], total)
            here = source[start : start + LANES, side * LANES : (side + 1) * LANES]
            total = total + skip_ref[...] * here.astype(f32)
            q, b = divmod(p, pieces)
            sums[q, b * LANES : (b + 1) * LANES, :] = total.astype(bf16)

        width = length + LANES
        for p in range(half // LANES):
            reach = (p + 1) * LANES
            within = jnp.dot(bands[:, width - reach :], source[0:reach, :], preferred_element_type=f32)
            across = jnp.dot(
                bands[:, width - reach - half : width - reach], source[:, 0:LANES], preferred_element_type=f32
            )
            finish(p, within[:, 0:LANES])
            finish(p + half // LANES, within[:, LANES:] + across)
        for q in range(n):
            if q == 0:
                tail = jnp.zeros((2, LANES), f32)
            else:
                tail = inputs[q - 1, block_len : block_len + EXTRA, :].astype(f32)[20:22]
            sums[q, block_len:, :] = jnp.concatenate([tail, jnp.zeros((BACK - 2, LANES), f32)], axis=0).astype(bf16)
        for ref, k in zip(out_refs, distances):
            ref[...] = sums[lax.rem(z + k, n)]

    back = jax.ShapeDtypeStruct((block_len + BACK, LANES), bf16)
    scratch = [
        pltpu.VMEM((n, block_len + EXTRA, LANES), bf16),
        pltpu.VMEM((half, 2 * LANES), bf16),
        pltpu.VMEM((4 * LANES, length + LANES), bf16),
        pltpu.VMEM((n, block_len + BACK, LANES), bf16),
    ]
    return vmem_call(kernel, [back] * n, scratch, *chunks, first_tail, short_kernel, skip_gain)


def gate(sums, queries, short_kernel, out_projection=None, cost=0):
    block_len = sums[0].shape[0] - BACK
    n = len(sums)
    f32, bf16 = jnp.float32, jnp.bfloat16
    arrays = []
    for array, _ in queries:
        if not any(array is a for a in arrays):
            arrays.append(array)
    places = [([a is array for a in arrays].index(True), index) for array, index in queries]

    masks = [()] if out_projection is None else [(2, 3), (1,)]

    def kernel(*refs):
        sum_refs, query_refs = refs[:n], refs[n : n + len(arrays)]
        short_ref, w_refs, out_refs = refs[n + len(arrays)], refs[n + len(arrays) + 1 : -len(masks)], refs[-len(masks) :]
        me = lax.axis_index("chan")
        for ref, targets in zip(out_refs, masks):
            for i, mask in enumerate(targets):
                first = pl.multiple_of(jnp.bitwise_xor(me, mask) * LANES, LANES)
                start = n * block_len + i * LANES
                ref[start : start + LANES, :] = w_refs[0][:, pl.ds(first, LANES)]
        for i, (a, index) in enumerate(places):
            tail = sum_refs[i][block_len:, :].astype(f32)
            k1, k2 = short_ref[1, 0:1, :], short_ref[2, 0:1, :]
            rim = [k1 * tail[1:2] + k2 * tail[0:1], k2 * tail[1:2], jnp.zeros((6, LANES), f32)]
            query = query_refs[a][index]
            query = jnp.concatenate([query[0:8] + jnp.concatenate(rim, axis=0), query[8:]], axis=0)
            out = query * sum_refs[i][0:block_len, :].astype(f32)
            for ref in out_refs:
                ref[i * block_len : (i + 1) * block_len, :] = out.astype(bf16)

    outs = [jax.ShapeDtypeStruct((n * block_len + len(m) * LANES, LANES), bf16) for m in masks]
    extra = [] if out_projection is None else [out_projection]
    return vmem_call(kernel, outs, [], *sums, *arrays, short_kernel, *extra, cost=cost)


def mix_early(slabs, out_projection, block_len):
    f32, bf16 = jnp.float32, jnp.bfloat16
    groups = len(slabs)
    counts = [slab[0].shape[0] // block_len for slab in slabs]
    counts[0] = 1

    def kernel(*refs):
        slab_refs, (w_ref, out_ref, w_all) = refs[: 4 * groups], refs[4 * groups :]
        me = lax.axis_index("chan")
        w_all[0:LANES, :] = w_ref[:, pl.ds(pl.multiple_of(me * LANES, LANES), LANES)]
        w_all[LANES : 2 * LANES, :] = slab_refs[1][block_len : block_len + LANES, :]
        w_all[2 * LANES : 3 * LANES, :] = slab_refs[2][block_len : block_len + LANES, :]
        w_all[3 * LANES :, :] = slab_refs[3][block_len + LANES : block_len + 2 * LANES, :]
        n = 0
        for g in range(groups):
            for i in range(counts[g]):
                rows = slice(i * block_len, (i + 1) * block_len)
                lhs = jnp.concatenate([ref[rows, :] for ref in slab_refs[4 * g : 4 * g + 4]], axis=1)
                out_ref[n] = jnp.dot(lhs, w_all[...], preferred_element_type=f32).astype(bf16)
                n += 1

    operands = [x for slab in slabs for x in slab] + [out_projection]
    outs = [VMEM((sum(counts), block_len, LANES), bf16), VMEM((4 * LANES, LANES), bf16)]
    return vmem_call(kernel, outs, [], *operands)


def mix_last(slab, columns, early, places, count):
    block_len = slab[0].shape[0]

    def kernel(*refs):
        slab_refs, (w_ref, early_ref, out_ref, last, sems) = refs[:4], refs[4:]
        z = lax.axis_index("seq")
        copies = []
        for i, k in enumerate(places):
            source = early_ref.at[i] if i < count - 1 else last
            copies.append(pltpu.make_async_copy(source, out_ref.at[lax.rem(z + k, count)], sems.at[i]))
        for copy in copies[:-1]:
            copy.start()
        lhs = jnp.concatenate([ref[...] for ref in slab_refs], axis=1)
        last[...] = jnp.dot(lhs, w_ref[...], preferred_element_type=jnp.float32).astype(jnp.bfloat16)
        copies[-1].start()
        for copy in copies:
            copy.wait()

    return pl.pallas_call(
        kernel,
        out_shape=jax.ShapeDtypeStruct((count, block_len, LANES), jnp.bfloat16),
        in_specs=[pl.BlockSpec(memory_space=VMEM)] * 6,
        out_specs=pl.BlockSpec(memory_space=pl.ANY),
        scratch_shapes=[pltpu.VMEM((block_len, LANES), jnp.bfloat16), pltpu.SemaphoreType.DMA((count,))],
        compiler_params=pltpu.CompilerParams(vmem_limit_bytes=GRANT),
        cost_estimate=NO_COST,
    )(*slab, columns, early)


def exchange_body(records, norm_gain, in_projection, short_kernel, long_filter, skip_gain, out_projection):
    block_len = records.shape[1]
    weights = jnp.transpose(in_projection, (1, 0, 2))
    gain = norm_gain.reshape(4, LANES)
    skip = skip_gain.reshape(1, LANES)

    (first,) = pick(records, ((2,),))
    second, third = pick(records, ((1, 3), (0,)))
    across_first, across_second, across_third = (exchange(block, "chan", 2) for block in (first, second, third))
    beside = exchange(after(records, first), "chan", 1)

    def projected(offsets, own, far, pieces):
        size = far.shape[0] // pieces
        diagonal = [exchange(far[i * size : (i + 1) * size], "chan", 1) for i in range(pieces)]
        return project(own, beside, far, diagonal, gain, weights, short_kernel, long_filter, offsets)

    (to_two,), query_two = projected((2,), first, across_first, 1)
    from_two = rotate(to_two, "seq", 2)
    (to_one, to_three), query_near = projected((1, 3), second, after(across_second, to_two), 2)
    from_one = rotate(to_one, "seq", 1)
    from_three = rotate(to_three, "seq", 3)
    (kept,), query_own = projected((0,), third, after(across_third, to_one), 1)

    tail, skip = tail_rows(from_two, skip, EARLY_COST)
    back_two, back_one, back_three, back_own = long_convolution(
        (from_two, from_one, from_three, kept), (2, 1, 3, 0), tail, short_kernel, skip
    )
    sums_two = rotate(back_two, "seq", 2)
    sums_one = rotate(back_one, "seq", 1)
    sums_three = rotate(back_three, "seq", 3)

    own, own_beside = gate([back_own], [(query_own, 0)], short_kernel, out_projection)
    own_over = exchange(own, "chan", 2)
    (near,) = gate([after(sums_one, own), after(sums_three, own)], [(query_near, 1), (query_near, 0)], short_kernel)
    near_over = exchange(near, "chan", 2)
    (far,) = gate([after(sums_two, near)], [(query_two, 0)], short_kernel, cost=FAR_COST)
    far = after(far, own_over)
    far_over = exchange(far, "chan", 2)

    def slab(gated, beside, over):
        return (gated, exchange(beside, "chan", 1), over, exchange(after(over, far), "chan", 1))

    early_slabs = [slab(own, own_beside, own_over), slab(near, near, near_over)]
    early, columns = mix_early(early_slabs, out_projection, block_len)
    return mix_last(slab(far, far, far_over), columns, early, (0, 3, 1, 2), records.shape[0])


def solution(mesh):
    placed = (
        P("parts", "seq", "chan"),
        P(),
        P(None, None, "chan"),
        P(None, None, "chan"),
        P("chan", "seq"),
        P("chan"),
        P("chan", None),
    )

    def body(records, norm_gain, in_projection, short_kernel, long_filter, skip_gain, out_projection):
        count, block_len, channels = records.shape
        fits = (
            count == 4
            and mesh.shape["seq"] == count
            and mesh.shape["chan"] == 4
            and channels == LANES
            and block_len == 3 * LANES
            and long_filter.shape[0] == 4
        )
        chosen = exchange_body if fits else ring_body
        return chosen(records, norm_gain, in_projection, short_kernel, long_filter, skip_gain, out_projection)

    return jax.shard_map(
        body, mesh=mesh, in_specs=placed, out_specs=P("parts", "seq", "chan"), check_vma=False
    )
```

```python
import jax
import jax.numpy as jnp
from jax import lax
from jax.experimental import pallas as pl
from jax.experimental.pallas import tpu as pltpu
from jax.sharding import PartitionSpec as P

LANES = 128
EXTRA = 32
NO_COST = pl.CostEstimate(flops=0, bytes_accessed=0, transcendentals=0)
EARLY_COST, FAR_COST = 1 << 30, 1 << 33
GRANT = 40 * 1024 * 1024
BACK = 16
VMEM = pltpu.VMEM


def from_behind(block, axis, distance):
    devices = range(lax.axis_size(axis))
    route = [(i - distance, i) for i in devices if i - distance in devices]
    return lax.ppermute(block, axis, route)


def block_terms(taps_padded, offset, block_source, block_len):
    filter_count = taps_padded.shape[0]
    window = lax.dynamic_slice_in_dim(taps_padded, offset + 1, 2 * block_len - 1, 1)
    flipped = window[:, ::-1]
    padded = jnp.pad(flipped, ((0, 0), (0, 1)))
    tiled_taps = jnp.tile(padded, (1, block_len))
    toeplitz = tiled_taps[:, block_len - 1 : block_len - 1 + block_len * (2 * block_len - 1)]
    toeplitz = toeplitz.reshape(filter_count, block_len, 2 * block_len - 1)[:, :, :block_len]
    record_count = block_source.shape[0]
    grouped = block_source.reshape(record_count, block_len, filter_count, -1)
    return jnp.einsum("fab,rbfg->rafg", toeplitz, grouped, preferred_element_type=jnp.float32)


def ring_body(records, norm_gain, in_projection, short_kernel, long_filter, skip_gain, out_projection):
    gathered = lax.all_gather(records, "chan", axis=2, tiled=True)
    widened = gathered.astype(jnp.float32)
    inv_rms = lax.rsqrt(jnp.mean(widened * widened, axis=-1, keepdims=True) + 1e-06)
    normed = (widened * inv_rms * norm_gain).astype(jnp.bfloat16)
    projected = jnp.einsum(
        "rtd,dkc->rtkc", normed, in_projection, preferred_element_type=jnp.float32
    ).astype(jnp.bfloat16)
    rim_rows = from_behind(projected[:, -2:], "seq", 1)
    extended = jnp.concatenate([rim_rows, projected], axis=1).astype(jnp.float32)
    streams = (
        short_kernel[0] * extended[:, 2:]
        + short_kernel[1] * extended[:, 1:-1]
        + short_kernel[2] * extended[:, :-2]
    )
    query_gate = streams[:, :, 0]
    gated_source = (streams[:, :, 1] * streams[:, :, 2]).astype(jnp.bfloat16)
    record_count, block_len, channels = gated_source.shape
    all_taps = lax.all_gather(long_filter, "seq", axis=1, tiled=True)
    taps_padded = jnp.concatenate(
        [jnp.zeros((all_taps.shape[0], block_len), jnp.bfloat16), all_taps], axis=1
    )
    my_start = lax.axis_index("seq") * block_len
    cycle_stops = lax.axis_size("seq")
    long_sum = block_terms(taps_padded, 0, gated_source, block_len)

    def advance(stop_index, state):
        running_sum, visiting = state
        visiting = from_behind(visiting, "seq", 1)
        lag_start = stop_index * block_len
        running_sum = lax.cond(
            lag_start <= my_start,
            lambda running: running + block_terms(taps_padded, lag_start, visiting, block_len),
            lambda running: running,
            running_sum,
        )
        return (running_sum, visiting)

    long_sum, _ = lax.fori_loop(1, cycle_stops, advance, (long_sum, gated_source))
    long_out = long_sum.reshape(
        record_count, block_len, channels
    ) + skip_gain * gated_source.astype(jnp.float32)
    gated = (query_gate * long_out).astype(jnp.bfloat16)
    partial_terms = jnp.einsum(
        "rtc,cd->rtd", gated, out_projection, preferred_element_type=jnp.float32
    )
    return lax.psum_scatter(
        partial_terms.astype(jnp.bfloat16), "chan", scatter_dimension=2, tiled=True
    )


def rotate(block, axis, distance):
    n = lax.axis_size(axis)
    return lax.ppermute(block, axis, [(i, (i + distance) % n) for i in range(n)])


def exchange(block, axis, mask):
    return lax.ppermute(block, axis, [(i, i ^ mask) for i in range(lax.axis_size(axis))])


def vmem_call(kernel, outs, scratch, *operands, cost=0):
    return pl.pallas_call(
        kernel,
        out_shape=tuple(outs),
        in_specs=[pl.BlockSpec(memory_space=VMEM)] * len(operands),
        out_specs=tuple(pl.BlockSpec(memory_space=VMEM) for _ in outs),
        scratch_shapes=scratch,
        compiler_params=pltpu.CompilerParams(vmem_limit_bytes=GRANT),
        cost_estimate=pl.CostEstimate(flops=cost, bytes_accessed=0, transcendentals=0),
    )(*operands)


def after(value, *done):
    return lax.optimization_barrier((value, *done))[0]


def pick(records, groups):
    count, block_len, _ = records.shape
    flat = [len(group) * block_len for group in groups]

    def kernel(records_ref, *rest):
        out_refs, sems = rest[:-1], rest[-1]
        z = lax.axis_index("seq")
        copies = []
        for ref, group in zip(out_refs, groups):
            for i, k in enumerate(group):
                place = ref.at[pl.ds(i * block_len, block_len)]
                copies.append(
                    pltpu.make_async_copy(records_ref.at[lax.rem(z + k, count)], place, sems.at[len(copies)])
                )
        for copy in copies:
            copy.start()
        for copy in copies:
            copy.wait()

    shapes = [VMEM((n, LANES), records.dtype) for n in flat]
    return pl.pallas_call(
        kernel,
        out_shape=tuple(shapes),
        in_specs=[pl.BlockSpec(memory_space=pl.ANY)],
        out_specs=tuple(pl.BlockSpec(memory_space=VMEM) for _ in shapes),
        scratch_shapes=[pltpu.SemaphoreType.DMA((count,))],
        cost_estimate=NO_COST,
    )(records)


def project(own, beside, across, diagonal, norm_gain, weights, short_kernel, taps, offsets):
    count, block_len, _ = beside.shape
    picked = len(offsets)
    depth = weights.shape[1]
    f32, bf16 = jnp.float32, jnp.bfloat16

    def kernel(own_ref, beside_ref, across_ref, gain_ref, w_ref, short_ref, taps_ref, *rest):
        diagonal_refs, rest = rest[: len(diagonal)], rest[len(diagonal) :]
        chunk_refs, (query_ref, w_all, shifted) = rest[:picked], rest[picked:]
        per = len(diagonal) // picked
        me = lax.axis_index("chan")
        z = lax.axis_index("seq")
        for j in range(4):
            first = pl.multiple_of(jnp.bitwise_xor(me, j) * LANES, LANES)
            for s in range(3):
                w_all[j * LANES : (j + 1) * LANES, s * LANES : (s + 1) * LANES] = w_ref[s, pl.ds(first, LANES), :]
        shifted[0:8, :] = jnp.zeros((8, 3 * LANES), f32)
        taps_block = taps_ref[...]
        flip = (
            lax.broadcasted_iota(jnp.int32, (LANES, LANES), 0)
            + lax.broadcasted_iota(jnp.int32, (LANES, LANES), 1)
            == LANES - 1
        ).astype(bf16)
        tap_rows = [
            jnp.dot(taps_block[:, b * LANES : (b + 1) * LANES], flip, preferred_element_type=f32)
            for b in range(block_len // LANES)
        ]
        for i, k in enumerate(offsets):
            rec = lax.rem(z + k, count)
            rows = slice(i * block_len, (i + 1) * block_len)
            pieces = [ref[...] for ref in diagonal_refs[i * per : (i + 1) * per]]
            slabs = [own_ref[rows, :], beside_ref[rec], across_ref[rows, :], jnp.concatenate(pieces, axis=0)]
            slabs = [s.astype(f32) for s in slabs]
            squares = slabs[0] * slabs[0]
            for s in slabs[1:]:
                squares = squares + s * s
            inv_rms = lax.rsqrt(jnp.sum(squares, axis=1, keepdims=True) * (1.0 / depth) + 1e-06)
            normed = [
                (s * inv_rms * gain_ref[pl.ds(jnp.bitwise_xor(me, j), 1), :]).astype(bf16)
                for j, s in enumerate(slabs)
            ]
            projected = jnp.dot(jnp.concatenate(normed, axis=1), w_all[...], preferred_element_type=f32)
            shifted[8:, :] = projected.astype(bf16).astype(f32)
            streams = []
            for s in range(3):
                cols = slice(s * LANES, (s + 1) * LANES)
                streams.append(
                    short_ref[0, s : s + 1, :] * shifted[8 : 8 + block_len, cols]
                    + short_ref[1, s : s + 1, :] * shifted[7 : 7 + block_len, cols]
                    + short_ref[2, s : s + 1, :] * shifted[6 : 6 + block_len, cols]
                )
            query_ref[i] = streams[0]
            chunk_refs[i][0:block_len, :] = (streams[1] * streams[2]).astype(bf16)
            heads = shifted[8:10, LANES:]
            tails = shifted[6 + block_len : 8 + block_len, :]
            rim = [heads[:, :LANES], heads[:, LANES:], tails[:, LANES : 2 * LANES], tails[:, 2 * LANES :], tails[:, :LANES]]
            extra = jnp.concatenate(tap_rows + rim + [jnp.zeros((EXTRA - 22, LANES), f32)], axis=0)
            chunk_refs[i][block_len:, :] = extra.astype(bf16)

    chunk = jax.ShapeDtypeStruct((block_len + EXTRA, LANES), bf16)
    query = jax.ShapeDtypeStruct((picked, block_len, LANES), f32)
    scratch = [pltpu.VMEM((4 * LANES, 3 * LANES), bf16), pltpu.VMEM((8 + block_len, 3 * LANES), f32)]
    out = vmem_call(
        kernel, [chunk] * picked + [query], scratch,
        own, beside, across, norm_gain, weights, short_kernel, taps, *diagonal,
    )
    return out[:picked], out[picked]


def tail_rows(block, skip_gain, cost):
    def kernel(block_ref, skip_ref, out_ref, same_ref):
        out_ref[...] = block_ref[-EXTRA:, :]
        same_ref[...] = skip_ref[...]

    outs = [jax.ShapeDtypeStruct((EXTRA, LANES), block.dtype), jax.ShapeDtypeStruct(skip_gain.shape, skip_gain.dtype)]
    return vmem_call(kernel, outs, [], block, skip_gain, cost=cost)


def long_convolution(chunks, distances, first_tail, short_kernel, skip_gain):
    n = len(chunks)
    block_len = chunks[0].shape[0] - EXTRA
    length = n * block_len
    half = length // 2
    pieces = block_len // LANES
    f32, bf16 = jnp.float32, jnp.bfloat16

    def kernel(*refs):
        chunk_refs, (tail_ref, short_ref, skip_ref), out_refs = refs[:n], refs[n : n + 3], refs[n + 3 : 2 * n + 3]
        inputs, source, bands, sums = refs[2 * n + 3 :]
        z = lax.axis_index("seq")
        for ref, k in zip(chunk_refs, distances):
            inputs[lax.rem(z - k + n, n)] = ref[...]
        inputs[lax.rem(z - distances[0] + n, n), block_len:, :] = tail_ref[...]
        lane = lax.broadcasted_iota(jnp.int32, (LANES, LANES), 1)
        tap_rows = [inputs[q, block_len : block_len + 4 * pieces, :].astype(f32) for q in range(n)]
        for f in range(4):
            row = [
                tap_rows[q][4 * b + f : 4 * b + f + 1, :] for q in reversed(range(n)) for b in reversed(range(pieces))
            ]
            row = jnp.concatenate(row + [jnp.zeros((1, LANES), f32)], axis=1)
            wide = jnp.broadcast_to(row, (LANES, length + LANES))
            band = pltpu.roll(wide, 1, 1, stride=1, stride_axis=0)
            bands[f * LANES : (f + 1) * LANES, :] = band.astype(bf16)
        short = [[short_ref[j, s : s + 1, :] for j in range(3)] for s in range(3)]
        for q in range(n):
            side, start = divmod(q * block_len, half)
            columns = slice(side * LANES, (side + 1) * LANES)
            source[start : start + block_len, columns] = inputs[q, :block_len, :]
            if q == 0:
                continue
            here = inputs[q, block_len : block_len + EXTRA, :].astype(f32)[4 * pieces :]
            past = inputs[q - 1, block_len : block_len + EXTRA, :].astype(f32)[4 * pieces :]
            fixed = []
            for s in (1, 2):
                head, tail = here[2 * s - 2 : 2 * s], past[2 * s + 2 : 2 * s + 4]
                k0, k1, k2 = short[s]
                fixed.append(
                    (
                        k0 * head[0:1] + k1 * tail[1:2] + k2 * tail[0:1],
                        k0 * head[1:2] + k1 * head[0:1] + k2 * tail[1:2],
                    )
                )
            first = inputs[q, 0:16, :].astype(f32)
            first = jnp.concatenate([fixed[0][t] * fixed[1][t] for t in range(2)] + [first[2:]], axis=0)
            source[start : start + 16, columns] = first.astype(bf16)

        def finish(p, terms):
            side, start = divmod(p * LANES, half)
            total = terms[0:LANES]
            for f in range(1, 4):
                total = jnp.where(lane >= f * 32, terms[f * LANES : (f + 1) * LANES], total)
            here = source[start : start + LANES, side * LANES : (side + 1) * LANES]
            total = total + skip_ref[...] * here.astype(f32)
            q, b = divmod(p, pieces)
            sums[q, b * LANES : (b + 1) * LANES, :] = total.astype(bf16)

        width = length + LANES
        pair = 2 * LANES
        pairs = half // pair
        crossed = [[None, None] for _ in range(pairs)]
        for lag in range(1, 2 * pairs):
            blocks = [q for q in range(pairs) if 0 <= lag - pairs + q < pairs]
            side = jnp.concatenate([source[q * pair : (q + 1) * pair, 0:LANES] for q in blocks], axis=1)
            for h in range(2):
                start = length - lag * pair - h * LANES
                terms = jnp.dot(bands[:, start : start + pair], side, preferred_element_type=f32)
                for i, q in enumerate(blocks):
                    part, place = terms[:, i * LANES : (i + 1) * LANES], crossed[lag - pairs + q]
                    place[h] = part if place[h] is None else place[h] + part
        for p in range(half // LANES):
            reach = (p + 1) * LANES
            within = jnp.dot(bands[:, width - reach :], source[0:reach, :], preferred_element_type=f32)
            finish(p, within[:, 0:LANES])
            finish(p + half // LANES, within[:, LANES:] + crossed[p // 2][p % 2])
        for q in range(n):
            if q == 0:
                tail = jnp.zeros((2, LANES), f32)
            else:
                tail = inputs[q - 1, block_len : block_len + EXTRA, :].astype(f32)[20:22]
            sums[q, block_len:, :] = jnp.concatenate([tail, jnp.zeros((BACK - 2, LANES), f32)], axis=0).astype(bf16)
        for ref, k in zip(out_refs, distances):
            ref[...] = sums[lax.rem(z + k, n)]

    back = jax.ShapeDtypeStruct((block_len + BACK, LANES), bf16)
    scratch = [
        pltpu.VMEM((n, block_len + EXTRA, LANES), bf16),
        pltpu.VMEM((half, 2 * LANES), bf16),
        pltpu.VMEM((4 * LANES, length + LANES), bf16),
        pltpu.VMEM((n, block_len + BACK, LANES), bf16),
    ]
    return vmem_call(kernel, [back] * n, scratch, *chunks, first_tail, short_kernel, skip_gain)


def gate(sums, queries, short_kernel, out_projection=None, cost=0):
    block_len = sums[0].shape[0] - BACK
    n = len(sums)
    f32, bf16 = jnp.float32, jnp.bfloat16
    arrays = []
    for array, _ in queries:
        if not any(array is a for a in arrays):
            arrays.append(array)
    places = [([a is array for a in arrays].index(True), index) for array, index in queries]

    masks = [()] if out_projection is None else [(2, 3), (1,)]

    def kernel(*refs):
        sum_refs, query_refs = refs[:n], refs[n : n + len(arrays)]
        short_ref, w_refs, out_refs = refs[n + len(arrays)], refs[n + len(arrays) + 1 : -len(masks)], refs[-len(masks) :]
        me = lax.axis_index("chan")
        for ref, targets in zip(out_refs, masks):
            for i, mask in enumerate(targets):
                first = pl.multiple_of(jnp.bitwise_xor(me, mask) * LANES, LANES)
                start = n * block_len + i * LANES
                ref[start : start + LANES, :] = w_refs[0][:, pl.ds(first, LANES)]
        for i, (a, index) in enumerate(places):
            tail = sum_refs[i][block_len:, :].astype(f32)
            k1, k2 = short_ref[1, 0:1, :], short_ref[2, 0:1, :]
            rim = [k1 * tail[1:2] + k2 * tail[0:1], k2 * tail[1:2], jnp.zeros((6, LANES), f32)]
            query = query_refs[a][index]
            query = jnp.concatenate([query[0:8] + jnp.concatenate(rim, axis=0), query[8:]], axis=0)
            out = query * sum_refs[i][0:block_len, :].astype(f32)
            for ref in out_refs:
                ref[i * block_len : (i + 1) * block_len, :] = out.astype(bf16)

    outs = [jax.ShapeDtypeStruct((n * block_len + len(m) * LANES, LANES), bf16) for m in masks]
    extra = [] if out_projection is None else [out_projection]
    return vmem_call(kernel, outs, [], *sums, *arrays, short_kernel, *extra, cost=cost)


def mix_early(slabs, out_projection, block_len):
    f32, bf16 = jnp.float32, jnp.bfloat16
    groups = len(slabs)
    counts = [slab[0].shape[0] // block_len for slab in slabs]
    counts[0] = 1

    def kernel(*refs):
        slab_refs, (w_ref, out_ref, w_all) = refs[: 4 * groups], refs[4 * groups :]
        me = lax.axis_index("chan")
        w_all[0:LANES, :] = w_ref[:, pl.ds(pl.multiple_of(me * LANES, LANES), LANES)]
        w_all[LANES : 2 * LANES, :] = slab_refs[1][block_len : block_len + LANES, :]
        w_all[2 * LANES : 3 * LANES, :] = slab_refs[2][block_len : block_len + LANES, :]
        w_all[3 * LANES :, :] = slab_refs[3][block_len + LANES : block_len + 2 * LANES, :]
        n = 0
        for g in range(groups):
            for i in range(counts[g]):
                rows = slice(i * block_len, (i + 1) * block_len)
                lhs = jnp.concatenate([ref[rows, :] for ref in slab_refs[4 * g : 4 * g + 4]], axis=1)
                out_ref[n] = jnp.dot(lhs, w_all[...], preferred_element_type=f32).astype(bf16)
                n += 1

    operands = [x for slab in slabs for x in slab] + [out_projection]
    outs = [VMEM((sum(counts), block_len, LANES), bf16), VMEM((4 * LANES, LANES), bf16)]
    return vmem_call(kernel, outs, [], *operands)


def mix_last(slab, columns, early, places, count):
    block_len = slab[0].shape[0]

    def kernel(*refs):
        slab_refs, (w_ref, early_ref, out_ref, last, sems) = refs[:4], refs[4:]
        z = lax.axis_index("seq")
        copies = []
        for i, k in enumerate(places):
            source = early_ref.at[i] if i < count - 1 else last
            copies.append(pltpu.make_async_copy(source, out_ref.at[lax.rem(z + k, count)], sems.at[i]))
        for copy in copies[:-1]:
            copy.start()
        lhs = jnp.concatenate([ref[...] for ref in slab_refs], axis=1)
        last[...] = jnp.dot(lhs, w_ref[...], preferred_element_type=jnp.float32).astype(jnp.bfloat16)
        copies[-1].start()
        for copy in copies:
            copy.wait()

    return pl.pallas_call(
        kernel,
        out_shape=jax.ShapeDtypeStruct((count, block_len, LANES), jnp.bfloat16),
        in_specs=[pl.BlockSpec(memory_space=VMEM)] * 6,
        out_specs=pl.BlockSpec(memory_space=pl.ANY),
        scratch_shapes=[pltpu.VMEM((block_len, LANES), jnp.bfloat16), pltpu.SemaphoreType.DMA((count,))],
        compiler_params=pltpu.CompilerParams(vmem_limit_bytes=GRANT),
        cost_estimate=NO_COST,
    )(*slab, columns, early)


def exchange_body(records, norm_gain, in_projection, short_kernel, long_filter, skip_gain, out_projection):
    block_len = records.shape[1]
    weights = jnp.transpose(in_projection, (1, 0, 2))
    gain = norm_gain.reshape(4, LANES)
    skip = skip_gain.reshape(1, LANES)

    (first,) = pick(records, ((2,),))
    second, third = pick(records, ((1, 3), (0,)))
    across_first, across_second, across_third = (exchange(block, "chan", 2) for block in (first, second, third))
    beside = exchange(after(records, first), "chan", 1)

    def projected(offsets, own, far, pieces):
        size = far.shape[0] // pieces
        diagonal = [exchange(far[i * size : (i + 1) * size], "chan", 1) for i in range(pieces)]
        return project(own, beside, far, diagonal, gain, weights, short_kernel, long_filter, offsets)

    (to_two,), query_two = projected((2,), first, across_first, 1)
    from_two = rotate(to_two, "seq", 2)
    (to_one, to_three), query_near = projected((1, 3), second, after(across_second, to_two), 2)
    from_one = rotate(to_one, "seq", 1)
    from_three = rotate(to_three, "seq", 3)
    (kept,), query_own = projected((0,), third, after(across_third, to_one), 1)

    tail, skip = tail_rows(from_two, skip, EARLY_COST)
    back_two, back_one, back_three, back_own = long_convolution(
        (from_two, from_one, from_three, kept), (2, 1, 3, 0), tail, short_kernel, skip
    )
    sums_two = rotate(back_two, "seq", 2)
    sums_one = rotate(back_one, "seq", 1)
    sums_three = rotate(back_three, "seq", 3)

    own, own_beside = gate([back_own], [(query_own, 0)], short_kernel, out_projection)
    own_over = exchange(own, "chan", 2)
    (near,) = gate([after(sums_one, own), after(sums_three, own)], [(query_near, 1), (query_near, 0)], short_kernel)
    near_over = exchange(near, "chan", 2)
    (far,) = gate([after(sums_two, near)], [(query_two, 0)], short_kernel, cost=FAR_COST)
    far = after(far, own_over)
    far_over = exchange(far, "chan", 2)

    def slab(gated, beside, over):
        return (gated, exchange(beside, "chan", 1), over, exchange(after(over, far), "chan", 1))

    early_slabs = [slab(own, own_beside, own_over), slab(near, near, near_over)]
    early, columns = mix_early(early_slabs, out_projection, block_len)
    return mix_last(slab(far, far, far_over), columns, early, (0, 3, 1, 2), records.shape[0])


def solution(mesh):
    placed = (
        P("parts", "seq", "chan"),
        P(),
        P(None, None, "chan"),
        P(None, None, "chan"),
        P("chan", "seq"),
        P("chan"),
        P("chan", None),
    )

    def body(records, norm_gain, in_projection, short_kernel, long_filter, skip_gain, out_projection):
        count, block_len, channels = records.shape
        fits = (
            count == 4
            and mesh.shape["seq"] == count
            and mesh.shape["chan"] == 4
            and channels == LANES
            and block_len == 3 * LANES
            and long_filter.shape[0] == 4
        )
        chosen = exchange_body if fits else ring_body
        return chosen(records, norm_gain, in_projection, short_kernel, long_filter, skip_gain, out_projection)

    return jax.shard_map(
        body, mesh=mesh, in_specs=placed, out_specs=P("parts", "seq", "chan"), check_vma=False
    )
```

```python
import jax
import jax.numpy as jnp
from jax import lax
from jax.experimental import pallas as pl
from jax.experimental.pallas import tpu as pltpu
from jax.sharding import PartitionSpec as P

LANES = 128
EXTRA = 32
NO_COST = pl.CostEstimate(flops=0, bytes_accessed=0, transcendentals=0)
EARLY_COST, FAR_COST = 1 << 30, 1 << 33
GRANT = 40 * 1024 * 1024
BACK = 16
VMEM = pltpu.VMEM


def from_behind(block, axis, distance):
    devices = range(lax.axis_size(axis))
    route = [(i - distance, i) for i in devices if i - distance in devices]
    return lax.ppermute(block, axis, route)


def block_terms(taps_padded, offset, block_source, block_len):
    filter_count = taps_padded.shape[0]
    window = lax.dynamic_slice_in_dim(taps_padded, offset + 1, 2 * block_len - 1, 1)
    flipped = window[:, ::-1]
    padded = jnp.pad(flipped, ((0, 0), (0, 1)))
    tiled_taps = jnp.tile(padded, (1, block_len))
    toeplitz = tiled_taps[:, block_len - 1 : block_len - 1 + block_len * (2 * block_len - 1)]
    toeplitz = toeplitz.reshape(filter_count, block_len, 2 * block_len - 1)[:, :, :block_len]
    record_count = block_source.shape[0]
    grouped = block_source.reshape(record_count, block_len, filter_count, -1)
    return jnp.einsum("fab,rbfg->rafg", toeplitz, grouped, preferred_element_type=jnp.float32)


def ring_body(records, norm_gain, in_projection, short_kernel, long_filter, skip_gain, out_projection):
    gathered = lax.all_gather(records, "chan", axis=2, tiled=True)
    widened = gathered.astype(jnp.float32)
    inv_rms = lax.rsqrt(jnp.mean(widened * widened, axis=-1, keepdims=True) + 1e-06)
    normed = (widened * inv_rms * norm_gain).astype(jnp.bfloat16)
    projected = jnp.einsum(
        "rtd,dkc->rtkc", normed, in_projection, preferred_element_type=jnp.float32
    ).astype(jnp.bfloat16)
    rim_rows = from_behind(projected[:, -2:], "seq", 1)
    extended = jnp.concatenate([rim_rows, projected], axis=1).astype(jnp.float32)
    streams = (
        short_kernel[0] * extended[:, 2:]
        + short_kernel[1] * extended[:, 1:-1]
        + short_kernel[2] * extended[:, :-2]
    )
    query_gate = streams[:, :, 0]
    gated_source = (streams[:, :, 1] * streams[:, :, 2]).astype(jnp.bfloat16)
    record_count, block_len, channels = gated_source.shape
    all_taps = lax.all_gather(long_filter, "seq", axis=1, tiled=True)
    taps_padded = jnp.concatenate(
        [jnp.zeros((all_taps.shape[0], block_len), jnp.bfloat16), all_taps], axis=1
    )
    my_start = lax.axis_index("seq") * block_len
    cycle_stops = lax.axis_size("seq")
    long_sum = block_terms(taps_padded, 0, gated_source, block_len)

    def advance(stop_index, state):
        running_sum, visiting = state
        visiting = from_behind(visiting, "seq", 1)
        lag_start = stop_index * block_len
        running_sum = lax.cond(
            lag_start <= my_start,
            lambda running: running + block_terms(taps_padded, lag_start, visiting, block_len),
            lambda running: running,
            running_sum,
        )
        return (running_sum, visiting)

    long_sum, _ = lax.fori_loop(1, cycle_stops, advance, (long_sum, gated_source))
    long_out = long_sum.reshape(
        record_count, block_len, channels
    ) + skip_gain * gated_source.astype(jnp.float32)
    gated = (query_gate * long_out).astype(jnp.bfloat16)
    partial_terms = jnp.einsum(
        "rtc,cd->rtd", gated, out_projection, preferred_element_type=jnp.float32
    )
    return lax.psum_scatter(
        partial_terms.astype(jnp.bfloat16), "chan", scatter_dimension=2, tiled=True
    )


def rotate(block, axis, distance):
    n = lax.axis_size(axis)
    return lax.ppermute(block, axis, [(i, (i + distance) % n) for i in range(n)])


def exchange(block, axis, mask):
    return lax.ppermute(block, axis, [(i, i ^ mask) for i in range(lax.axis_size(axis))])


def vmem_call(kernel, outs, scratch, *operands, cost=0):
    return pl.pallas_call(
        kernel,
        out_shape=tuple(outs),
        in_specs=[pl.BlockSpec(memory_space=VMEM)] * len(operands),
        out_specs=tuple(pl.BlockSpec(memory_space=VMEM) for _ in outs),
        scratch_shapes=scratch,
        compiler_params=pltpu.CompilerParams(vmem_limit_bytes=GRANT),
        cost_estimate=pl.CostEstimate(flops=cost, bytes_accessed=0, transcendentals=0),
    )(*operands)


def after(value, *done):
    return lax.optimization_barrier((value, *done))[0]


def reversed_rows(taps):
    row = lax.broadcasted_iota(jnp.int32, (LANES, LANES), 0)
    column = lax.broadcasted_iota(jnp.int32, (LANES, LANES), 1)
    flip = (row + column == LANES - 1).astype(taps.dtype)
    return [
        jnp.dot(taps[:, b * LANES : (b + 1) * LANES], flip, preferred_element_type=jnp.float32)
        for b in range(taps.shape[1] // LANES)
    ]


def pick(records, groups, taps=None):
    count, block_len, _ = records.shape
    with_taps = taps is not None

    def kernel(records_ref, *rest):
        taps_ref, rest = (rest[0], rest[1:]) if with_taps else (None, rest)
        out_refs, rest = rest[: len(groups)], rest[len(groups) :]
        sems = rest[-1]
        z = lax.axis_index("seq")
        copies = []
        for ref, group in zip(out_refs, groups):
            for i, k in enumerate(group):
                place = ref.at[pl.ds(i * block_len, block_len)]
                copies.append(
                    pltpu.make_async_copy(records_ref.at[lax.rem(z + k, count)], place, sems.at[len(copies)])
                )
        for copy in copies:
            copy.start()
        if with_taps:
            rows_ref, held = rest[0], rest[1]
            fetch = pltpu.make_async_copy(taps_ref, held, sems.at[len(copies)])
            fetch.start()
            fetch.wait()
            rows_ref[...] = jnp.concatenate(reversed_rows(held[...]), axis=0)
        for copy in copies:
            copy.wait()

    shapes = [VMEM((len(group) * block_len, LANES), records.dtype) for group in groups]
    scratch = [pltpu.SemaphoreType.DMA((count + 1,))]
    operands = [records]
    if with_taps:
        shapes.append(VMEM((taps.size // LANES, LANES), jnp.float32))
        scratch.insert(0, pltpu.VMEM(taps.shape, taps.dtype))
        operands.append(taps)
    return pl.pallas_call(
        kernel,
        out_shape=tuple(shapes),
        in_specs=[pl.BlockSpec(memory_space=pl.ANY)] * len(operands),
        out_specs=tuple(pl.BlockSpec(memory_space=VMEM) for _ in shapes),
        scratch_shapes=scratch,
        cost_estimate=NO_COST,
    )(*operands)


def project(own, beside, across, diagonal, norm_gain, weights, short_kernel, taps, offsets):
    count, block_len, _ = beside.shape
    picked = len(offsets)
    depth = weights.shape[1]
    f32, bf16 = jnp.float32, jnp.bfloat16

    def kernel(own_ref, beside_ref, across_ref, gain_ref, w_ref, short_ref, taps_ref, *rest):
        diagonal_refs, rest = rest[: len(diagonal)], rest[len(diagonal) :]
        chunk_refs, (query_ref, w_all, shifted) = rest[:picked], rest[picked:]
        per = len(diagonal) // picked
        me = lax.axis_index("chan")
        z = lax.axis_index("seq")
        for j in range(4):
            first = pl.multiple_of(jnp.bitwise_xor(me, j) * LANES, LANES)
            for s in range(3):
                w_all[j * LANES : (j + 1) * LANES, s * LANES : (s + 1) * LANES] = w_ref[s, pl.ds(first, LANES), :]
        shifted[0:8, :] = jnp.zeros((8, 3 * LANES), f32)
        tap_rows = [taps_ref[...]]
        for i, k in enumerate(offsets):
            rec = lax.rem(z + k, count)
            rows = slice(i * block_len, (i + 1) * block_len)
            pieces = [ref[...] for ref in diagonal_refs[i * per : (i + 1) * per]]
            slabs = [own_ref[rows, :], beside_ref[rec], across_ref[rows, :], jnp.concatenate(pieces, axis=0)]
            slabs = [s.astype(f32) for s in slabs]
            squares = slabs[0] * slabs[0]
            for s in slabs[1:]:
                squares = squares + s * s
            inv_rms = lax.rsqrt(jnp.sum(squares, axis=1, keepdims=True) * (1.0 / depth) + 1e-06)
            normed = [
                (s * inv_rms * gain_ref[pl.ds(jnp.bitwise_xor(me, j), 1), :]).astype(bf16)
                for j, s in enumerate(slabs)
            ]
            projected = jnp.dot(jnp.concatenate(normed, axis=1), w_all[...], preferred_element_type=f32)
            shifted[8:, :] = projected.astype(bf16).astype(f32)
            streams = []
            for s in range(3):
                cols = slice(s * LANES, (s + 1) * LANES)
                streams.append(
                    short_ref[0, s : s + 1, :] * shifted[8 : 8 + block_len, cols]
                    + short_ref[1, s : s + 1, :] * shifted[7 : 7 + block_len, cols]
                    + short_ref[2, s : s + 1, :] * shifted[6 : 6 + block_len, cols]
                )
            query_ref[i] = streams[0]
            chunk_refs[i][0:block_len, :] = (streams[1] * streams[2]).astype(bf16)
            heads = shifted[8:10, LANES:]
            tails = shifted[6 + block_len : 8 + block_len, :]
            rim = [heads[:, :LANES], heads[:, LANES:], tails[:, LANES : 2 * LANES], tails[:, 2 * LANES :], tails[:, :LANES]]
            extra = jnp.concatenate(tap_rows + rim + [jnp.zeros((EXTRA - 22, LANES), f32)], axis=0)
            chunk_refs[i][block_len:, :] = extra.astype(bf16)

    chunk = jax.ShapeDtypeStruct((block_len + EXTRA, LANES), bf16)
    query = jax.ShapeDtypeStruct((picked, block_len, LANES), f32)
    scratch = [pltpu.VMEM((4 * LANES, 3 * LANES), bf16), pltpu.VMEM((8 + block_len, 3 * LANES), f32)]
    out = vmem_call(
        kernel, [chunk] * picked + [query], scratch,
        own, beside, across, norm_gain, weights, short_kernel, taps, *diagonal,
    )
    return out[:picked], out[picked]


def tail_rows(block, skip_gain, cost):
    def kernel(block_ref, skip_ref, out_ref, same_ref):
        out_ref[...] = block_ref[-EXTRA:, :]
        same_ref[...] = skip_ref[...]

    outs = [jax.ShapeDtypeStruct((EXTRA, LANES), block.dtype), jax.ShapeDtypeStruct(skip_gain.shape, skip_gain.dtype)]
    return vmem_call(kernel, outs, [], block, skip_gain, cost=cost)


def long_convolution(chunks, distances, first_tail, short_kernel, skip_gain):
    n = len(chunks)
    block_len = chunks[0].shape[0] - EXTRA
    length = n * block_len
    half = length // 2
    pieces = block_len // LANES
    f32, bf16 = jnp.float32, jnp.bfloat16

    def kernel(*refs):
        chunk_refs, (tail_ref, short_ref, skip_ref), out_refs = refs[:n], refs[n : n + 3], refs[n + 3 : 2 * n + 3]
        inputs, source, bands, sums = refs[2 * n + 3 :]
        z = lax.axis_index("seq")
        for ref, k in zip(chunk_refs, distances):
            inputs[lax.rem(z - k + n, n)] = ref[...]
        inputs[lax.rem(z - distances[0] + n, n), block_len:, :] = tail_ref[...]
        lane = lax.broadcasted_iota(jnp.int32, (LANES, LANES), 1)
        tap_rows = [inputs[q, block_len : block_len + 4 * pieces, :].astype(f32) for q in range(n)]
        for f in range(4):
            row = [
                tap_rows[q][4 * b + f : 4 * b + f + 1, :] for q in reversed(range(n)) for b in reversed(range(pieces))
            ]
            row = jnp.concatenate(row + [jnp.zeros((1, LANES), f32)], axis=1)
            wide = jnp.broadcast_to(row, (LANES, length + LANES))
            band = pltpu.roll(wide, 1, 1, stride=1, stride_axis=0)
            bands[f * LANES : (f + 1) * LANES, :] = band.astype(bf16)
        short = [[short_ref[j, s : s + 1, :] for j in range(3)] for s in range(3)]
        for q in range(n):
            side, start = divmod(q * block_len, half)
            columns = slice(side * LANES, (side + 1) * LANES)
            source[start : start + block_len, columns] = inputs[q, :block_len, :]
            if q == 0:
                continue
            here = inputs[q, block_len : block_len + EXTRA, :].astype(f32)[4 * pieces :]
            past = inputs[q - 1, block_len : block_len + EXTRA, :].astype(f32)[4 * pieces :]
            fixed = []
            for s in (1, 2):
                head, tail = here[2 * s - 2 : 2 * s], past[2 * s + 2 : 2 * s + 4]
                k0, k1, k2 = short[s]
                fixed.append(
                    (
                        k0 * head[0:1] + k1 * tail[1:2] + k2 * tail[0:1],
                        k0 * head[1:2] + k1 * head[0:1] + k2 * tail[1:2],
                    )
                )
            first = inputs[q, 0:16, :].astype(f32)
            first = jnp.concatenate([fixed[0][t] * fixed[1][t] for t in range(2)] + [first[2:]], axis=0)
            source[start : start + 16, columns] = first.astype(bf16)

        def finish(p, terms):
            side, start = divmod(p * LANES, half)
            total = terms[0:LANES]
            for f in range(1, 4):
                total = jnp.where(lane >= f * 32, terms[f * LANES : (f + 1) * LANES], total)
            here = source[start : start + LANES, side * LANES : (side + 1) * LANES]
            total = total + skip_ref[...] * here.astype(f32)
            q, b = divmod(p, pieces)
            sums[q, b * LANES : (b + 1) * LANES, :] = total.astype(bf16)

        width = length + LANES
        pair = 2 * LANES
        pairs = half // pair
        crossed = [[None, None] for _ in range(pairs)]
        for lag in range(1, 2 * pairs):
            blocks = [q for q in range(pairs) if 0 <= lag - pairs + q < pairs]
            side = jnp.concatenate([source[q * pair : (q + 1) * pair, 0:LANES] for q in blocks], axis=1)
            for h in range(2):
                start = length - lag * pair - h * LANES
                terms = jnp.dot(bands[:, start : start + pair], side, preferred_element_type=f32)
                for i, q in enumerate(blocks):
                    part, place = terms[:, i * LANES : (i + 1) * LANES], crossed[lag - pairs + q]
                    place[h] = part if place[h] is None else place[h] + part
        for p in range(half // LANES):
            reach = (p + 1) * LANES
            within = jnp.dot(bands[:, width - reach :], source[0:reach, :], preferred_element_type=f32)
            finish(p, within[:, 0:LANES])
            finish(p + half // LANES, within[:, LANES:] + crossed[p // 2][p % 2])
        for q in range(n):
            if q == 0:
                tail = jnp.zeros((2, LANES), f32)
            else:
                tail = inputs[q - 1, block_len : block_len + EXTRA, :].astype(f32)[20:22]
            sums[q, block_len:, :] = jnp.concatenate([tail, jnp.zeros((BACK - 2, LANES), f32)], axis=0).astype(bf16)
        for ref, k in zip(out_refs, distances):
            ref[...] = sums[lax.rem(z + k, n)]

    back = jax.ShapeDtypeStruct((block_len + BACK, LANES), bf16)
    scratch = [
        pltpu.VMEM((n, block_len + EXTRA, LANES), bf16),
        pltpu.VMEM((half, 2 * LANES), bf16),
        pltpu.VMEM((4 * LANES, length + LANES), bf16),
        pltpu.VMEM((n, block_len + BACK, LANES), bf16),
    ]
    return vmem_call(kernel, [back] * n, scratch, *chunks, first_tail, short_kernel, skip_gain)


def gate(sums, queries, short_kernel, out_projection=None, cost=0):
    block_len = sums[0].shape[0] - BACK
    n = len(sums)
    f32, bf16 = jnp.float32, jnp.bfloat16
    arrays = []
    for array, _ in queries:
        if not any(array is a for a in arrays):
            arrays.append(array)
    places = [([a is array for a in arrays].index(True), index) for array, index in queries]

    masks = [()] if out_projection is None else [(2, 3), (1,)]

    def kernel(*refs):
        sum_refs, query_refs = refs[:n], refs[n : n + len(arrays)]
        short_ref, w_refs, out_refs = refs[n + len(arrays)], refs[n + len(arrays) + 1 : -len(masks)], refs[-len(masks) :]
        me = lax.axis_index("chan")
        for ref, targets in zip(out_refs, masks):
            for i, mask in enumerate(targets):
                first = pl.multiple_of(jnp.bitwise_xor(me, mask) * LANES, LANES)
                start = n * block_len + i * LANES
                ref[start : start + LANES, :] = w_refs[0][:, pl.ds(first, LANES)]
        for i, (a, index) in enumerate(places):
            tail = sum_refs[i][block_len:, :].astype(f32)
            k1, k2 = short_ref[1, 0:1, :], short_ref[2, 0:1, :]
            rim = [k1 * tail[1:2] + k2 * tail[0:1], k2 * tail[1:2], jnp.zeros((6, LANES), f32)]
            query = query_refs[a][index]
            query = jnp.concatenate([query[0:8] + jnp.concatenate(rim, axis=0), query[8:]], axis=0)
            out = query * sum_refs[i][0:block_len, :].astype(f32)
            for ref in out_refs:
                ref[i * block_len : (i + 1) * block_len, :] = out.astype(bf16)

    outs = [jax.ShapeDtypeStruct((n * block_len + len(m) * LANES, LANES), bf16) for m in masks]
    extra = [] if out_projection is None else [out_projection]
    return vmem_call(kernel, outs, [], *sums, *arrays, short_kernel, *extra, cost=cost)


def mix_early(slabs, out_projection, block_len):
    f32, bf16 = jnp.float32, jnp.bfloat16
    groups = len(slabs)
    counts = [slab[0].shape[0] // block_len for slab in slabs]
    counts[0] = 1

    def kernel(*refs):
        slab_refs, (w_ref, out_ref, w_all) = refs[: 4 * groups], refs[4 * groups :]
        me = lax.axis_index("chan")
        w_all[0:LANES, :] = w_ref[:, pl.ds(pl.multiple_of(me * LANES, LANES), LANES)]
        w_all[LANES : 2 * LANES, :] = slab_refs[1][block_len : block_len + LANES, :]
        w_all[2 * LANES : 3 * LANES, :] = slab_refs[2][block_len : block_len + LANES, :]
        w_all[3 * LANES :, :] = slab_refs[3][block_len + LANES : block_len + 2 * LANES, :]
        n = 0
        for g in range(groups):
            for i in range(counts[g]):
                rows = slice(i * block_len, (i + 1) * block_len)
                lhs = jnp.concatenate([ref[rows, :] for ref in slab_refs[4 * g : 4 * g + 4]], axis=1)
                out_ref[n] = jnp.dot(lhs, w_all[...], preferred_element_type=f32).astype(bf16)
                n += 1

    operands = [x for slab in slabs for x in slab] + [out_projection]
    outs = [VMEM((sum(counts), block_len, LANES), bf16), VMEM((4 * LANES, LANES), bf16)]
    return vmem_call(kernel, outs, [], *operands)


def mix_last(slab, columns, early, places, count):
    block_len = slab[0].shape[0]

    def kernel(*refs):
        slab_refs, (w_ref, early_ref, out_ref, last, sems) = refs[:4], refs[4:]
        z = lax.axis_index("seq")
        copies = []
        for i, k in enumerate(places):
            source = early_ref.at[i] if i < count - 1 else last
            copies.append(pltpu.make_async_copy(source, out_ref.at[lax.rem(z + k, count)], sems.at[i]))
        for copy in copies[:-1]:
            copy.start()
        lhs = jnp.concatenate([ref[...] for ref in slab_refs], axis=1)
        last[...] = jnp.dot(lhs, w_ref[...], preferred_element_type=jnp.float32).astype(jnp.bfloat16)
        copies[-1].start()
        for copy in copies:
            copy.wait()

    return pl.pallas_call(
        kernel,
        out_shape=jax.ShapeDtypeStruct((count, block_len, LANES), jnp.bfloat16),
        in_specs=[pl.BlockSpec(memory_space=VMEM)] * 6,
        out_specs=pl.BlockSpec(memory_space=pl.ANY),
        scratch_shapes=[pltpu.VMEM((block_len, LANES), jnp.bfloat16), pltpu.SemaphoreType.DMA((count,))],
        compiler_params=pltpu.CompilerParams(vmem_limit_bytes=GRANT),
        cost_estimate=NO_COST,
    )(*slab, columns, early)


def exchange_body(records, norm_gain, in_projection, short_kernel, long_filter, skip_gain, out_projection):
    block_len = records.shape[1]
    weights = jnp.transpose(in_projection, (1, 0, 2))
    gain = norm_gain.reshape(4, LANES)
    skip = skip_gain.reshape(1, LANES)

    (first,) = pick(records, ((2,),))
    second, third, long_filter = pick(records, ((1, 3), (0,)), long_filter)
    across_first, across_second, across_third = (exchange(block, "chan", 2) for block in (first, second, third))
    beside = exchange(records, "chan", 1)

    def projected(offsets, own, far, pieces):
        size = far.shape[0] // pieces
        diagonal = [exchange(far[i * size : (i + 1) * size], "chan", 1) for i in range(pieces)]
        return project(own, beside, far, diagonal, gain, weights, short_kernel, long_filter, offsets)

    (to_two,), query_two = projected((2,), first, across_first, 1)
    from_two = rotate(to_two, "seq", 2)
    (to_one, to_three), query_near = projected((1, 3), second, after(across_second, to_two), 2)
    from_one = rotate(to_one, "seq", 1)
    from_three = rotate(to_three, "seq", 3)
    (kept,), query_own = projected((0,), third, after(across_third, to_one), 1)

    tail, skip = tail_rows(from_two, skip, EARLY_COST)
    back_two, back_one, back_three, back_own = long_convolution(
        (from_two, from_one, from_three, kept), (2, 1, 3, 0), tail, short_kernel, skip
    )
    sums_two = rotate(back_two, "seq", 2)
    sums_one = rotate(back_one, "seq", 1)
    sums_three = rotate(back_three, "seq", 3)

    own, own_beside = gate([back_own], [(query_own, 0)], short_kernel, out_projection)
    own_over = exchange(own, "chan", 2)
    (near,) = gate([after(sums_one, own), after(sums_three, own)], [(query_near, 1), (query_near, 0)], short_kernel)
    near_over = exchange(near, "chan", 2)
    (far,) = gate([after(sums_two, near)], [(query_two, 0)], short_kernel, cost=FAR_COST)
    far_over = exchange(far, "chan", 2)

    def slab(gated, beside, over):
        return (gated, exchange(beside, "chan", 1), over, exchange(after(over, far), "chan", 1))

    early_slabs = [slab(own, own_beside, own_over), slab(near, near, near_over)]
    early, columns = mix_early(early_slabs, out_projection, block_len)
    return mix_last(slab(far, far, far_over), columns, early, (0, 3, 1, 2), records.shape[0])


def solution(mesh):
    placed = (
        P("parts", "seq", "chan"),
        P(),
        P(None, None, "chan"),
        P(None, None, "chan"),
        P("chan", "seq"),
        P("chan"),
        P("chan", None),
    )

    def body(records, norm_gain, in_projection, short_kernel, long_filter, skip_gain, out_projection):
        count, block_len, channels = records.shape
        fits = (
            count == 4
            and mesh.shape["seq"] == count
            and mesh.shape["chan"] == 4
            and channels == LANES
            and block_len == 3 * LANES
            and long_filter.shape[0] == 4
        )
        chosen = exchange_body if fits else ring_body
        return chosen(records, norm_gain, in_projection, short_kernel, long_filter, skip_gain, out_projection)

    return jax.shard_map(
        body, mesh=mesh, in_specs=placed, out_specs=P("parts", "seq", "chan"), check_vma=False
    )
```
